256 devices in a mesh: src: 32 (over y, z), dst: 8 (over x, core).
Axes of the slice: x: 4, y: 4, z: 8, core: 2. Of those that a mesh axis runs over, the one named last changes fastest.
Arguments:
- features: bfloat16 [131072, 768], P(('dst', 'src')), may hold values from -300 to 300
- weight: bfloat16 [768, 256], replicated, may hold values from -0.21875 to 0.21875
- att_src: float32 [256], replicated, may hold values from -0.75 to 0.75
- att_dst: float32 [256], replicated, may hold values from -0.75 to 0.75
- bias: float32 [256], replicated, may hold values from -3 to 3
- block_pairs: int32 [32, 8, 32, 2], P('src', 'dst'), may hold values from 0 to 127, as said below
- edge_masks: int32 [32, 8, 32, 2, 128, 128], P('src', 'dst'), may hold values from 0 to 1, as said below
Outputs:
- output: float32 [131072, 256], P(('dst', 'src'))
The draws below stay inside these ranges and needn't reach their ends.
Inputs may be any that keep to these rules, and one draw needn't show every extreme that they name: `block_pairs`: the 2 entries of one device and one owner are distinct. `edge_masks`: every row of every listed block holds at least one edge.
All inputs are finite; a program needn't handle non-finite values.
Results may differ from the reference program's by a relative error of at most 0.039.
Values may be sent and summed in bfloat16 or wider, within the bound.
No kernel may reach another device: no remote copies, remote signals or barrier semaphores. Data moves between devices by JAX's collectives and lax.ppermute only.
A program may use at most 128 MiB of HBM per device.

```python
import jax
import jax.numpy as jnp
from jax import lax

IN = 768
HEADS = 4
HEAD = 64
BLK = 128
NBD = 4
OWNER_SLOTS = 2
SRC_BLOCKS = 32
DST_BLOCKS = 128
NODES = 131072
N_SRC = 32
N_DST = 8


def draw_features(key, part):
    shape = (NODES, IN)
    values = jnp.clip(jax.random.normal(jax.random.fold_in(key, 1), shape, jnp.float32), -6.0, 6.0)
    return values.astype(jnp.bfloat16)


def draw_block_pairs(key, part):
    lists = N_SRC * N_DST * N_SRC
    keys = jax.random.split(jax.random.fold_in(key, 21), lists)
    choose = jax.vmap(lambda single: jax.random.permutation(single, NBD * SRC_BLOCKS)[:OWNER_SLOTS])
    return choose(keys).astype(jnp.int32).reshape(N_SRC, N_DST, N_SRC, OWNER_SLOTS)


def draw_edge_masks(key, part):
    shape = (N_SRC, N_DST, N_SRC, OWNER_SLOTS, BLK, BLK)
    sparse = jax.random.randint(jax.random.fold_in(key, 33), shape, 0, 64) == 0
    column = jax.random.randint(jax.random.fold_in(key, 34), shape[:-1] + (1,), 0, BLK)
    forced = jnp.arange(BLK, dtype=jnp.int32) == column
    return (sparse | forced).astype(jnp.int32)


def gaussian(own_key, extent, width, limit, kind=jnp.bfloat16):
    array = width * jax.random.normal(own_key, extent, jnp.float32)
    return jnp.clip(array, min=-limit, max=limit).astype(kind)


def setup_inputs(seed: int = 0) -> dict:
    key_of = jax.random.split(jax.random.key(seed), 8)
    features = draw_features(jax.random.fold_in(key_of[7], 71), 0)
    weight = gaussian(key_of[1], (IN, HEADS * HEAD), IN ** -0.5, 0.21875)
    att_src = gaussian(key_of[2], (HEADS * HEAD,), HEAD ** -0.5, 0.75, jnp.float32)
    att_dst = gaussian(key_of[3], (HEADS * HEAD,), HEAD ** -0.5, 0.75, jnp.float32)
    bias = gaussian(key_of[4], (HEADS * HEAD,), 0.5, 3.0, jnp.float32)
    block_pairs = draw_block_pairs(jax.random.fold_in(key_of[7], 71), 0)
    edge_masks = draw_edge_masks(jax.random.fold_in(key_of[7], 71), 0)
    return {"features": features, "weight": weight, "att_src": att_src, "att_dst": att_dst, "bias": bias, "block_pairs": block_pairs, "edge_masks": edge_masks}


lowest = -1e30


def leaky(values):
    return jnp.where(values > 0, values, 0.2 * values)


def reference(features, weight, att_src, att_dst, bias, block_pairs, edge_masks):
    nodes = features.shape[0]
    blocks = nodes // BLK
    hidden = jnp.dot(features, weight, preferred_element_type=jnp.float32).astype(jnp.bfloat16)
    flat = hidden.astype(jnp.float32).reshape(nodes, HEADS, HEAD)
    source_score = jnp.einsum("nkc,kc->kn", flat, att_src.reshape(HEADS, HEAD))
    target_score = jnp.einsum("nkc,kc->kn", flat, att_dst.reshape(HEADS, HEAD))
    source_blocks = source_score.reshape(HEADS, blocks, BLK).transpose(1, 0, 2)
    target_blocks = target_score.reshape(HEADS, blocks, BLK).transpose(1, 0, 2)
    values = flat.reshape(blocks, BLK, HEADS, HEAD)
    self_logit = leaky(target_blocks + source_blocks)
    pairs = block_pairs.reshape(N_SRC * N_DST, N_SRC * OWNER_SLOTS)
    masks = edge_masks.reshape(N_SRC * N_DST, N_SRC * OWNER_SLOTS, BLK, BLK)
    counter = jnp.arange(N_SRC * N_DST, dtype=jnp.int32)
    source_group = counter // N_DST
    target_group = counter % N_DST
    owner = jnp.arange(N_SRC * OWNER_SLOTS, dtype=jnp.int32) // OWNER_SLOTS

    def scores(item):
        pair, mask, group_s, group_d = item
        dst_pick = group_d * DST_BLOCKS + owner * NBD + pair // SRC_BLOCKS
        local = pair % SRC_BLOCKS
        src_pick = (local // NBD) * DST_BLOCKS + group_s * NBD + local % NBD
        logits = leaky(target_blocks[dst_pick][:, :, :, None] + source_blocks[src_pick][:, :, None, :])
        live = (mask > 0)[:, None]
        return dst_pick, src_pick, jnp.where(live, logits, lowest), live

    def first_pass(bound, item):
        dst_pick, src_pick, logits, live = scores(item)
        return bound.at[dst_pick].max(logits.max(-1)), None

    bound, _ = lax.scan(first_pass, self_logit, (pairs, masks, source_group, target_group))

    def second_pass(carry, item):
        totals, accum = carry
        dst_pick, src_pick, logits, live = scores(item)
        weights = jnp.where(live, jnp.exp(logits - bound[dst_pick][..., None]), 0.0)
        rounded = lax.optimization_barrier(weights.astype(jnp.bfloat16)).astype(jnp.float32)
        numer = jnp.einsum("lkij,ljkc->lkci", rounded, values[src_pick])
        return (totals.at[dst_pick].add(weights.sum(-1)), accum.at[dst_pick].add(numer)), None

    keep = jnp.exp(self_logit - bound)
    start = (keep, values.transpose(0, 2, 3, 1) * keep[:, :, None, :])
    (totals, accum), _ = lax.scan(second_pass, start, (pairs, masks, source_group, target_group))
    result = (accum / totals[:, :, None, :]).transpose(0, 3, 1, 2).reshape(nodes, HEADS * HEAD) + bias
    return jax.nn.elu(result).astype(jnp.float32)
```

```python
import functools

import jax
import jax.numpy as jnp
from jax import lax
from jax.experimental import pallas as pl
from jax.experimental.pallas import tpu as pltpu
from jax.sharding import PartitionSpec as P

HEADS = 4
HEAD = 64
FEAT = HEADS * HEAD
BLK = 128
NBD = 4
SLOTS = 2
NY, NZ, NX, NC = 4, 8, 4, 2
PIECES = NX * NC
SRC_BLOCKS = NBD * PIECES
OWNERS = NY * NZ
PAIRS = OWNERS * SLOTS
ROWS = FEAT + 16
LOG2E = 1.4426950408889634
EMPTY = -(2.0**100)
GROUPS = NZ // 2
F32 = jnp.float32
BF16 = jnp.bfloat16
VMEM = pl.BlockSpec(memory_space=pltpu.VMEM)
ANY = pl.BlockSpec(memory_space=pl.ANY)


def params(**more):
    return pltpu.CompilerParams(vmem_limit_bytes=40 * 1024 * 1024, **more)


def leaky(values):
    return jnp.maximum(values, 0.2 * values)


def y_from(k):
    return [(y * NZ + z, (y - k) % NY * NZ + z) for y in range(NY) for z in range(NZ)]


def z_from(k):
    return [(y * NZ + z, y * NZ + (z - k) % NZ) for y in range(NY) for z in range(NZ)]


def x_from(k):
    return [(x * NC + c, (x - k) % NX * NC + c) for x in range(NX) for c in range(NC)]


def core_from(k):
    return [(x * NC + c, x * NC + (c - k) % NC) for x in range(NX) for c in range(NC)]


def up_offset(group):
    return NZ // 2 - group


def down_offset(group):
    return (NZ // 2 + 1 + group) % NZ


def head_sums(products):
    return jnp.concatenate(
        [jnp.sum(products[h * HEAD : (h + 1) * HEAD], axis=0, keepdims=True) for h in range(HEADS)],
        axis=0,
    )


def project_kernel(x_ref, w_ref, src_ref, dst_ref, hidden_ref, target_ref, self_ref, att_ref):
    att_src = jnp.broadcast_to(src_ref[...] * LOG2E, (BLK, FEAT)).T
    att_dst = jnp.broadcast_to(dst_ref[...] * LOG2E, (BLK, FEAT)).T
    att_ref[...] = att_src
    for b in range(NBD):
        hidden = jnp.dot(
            x_ref[b * BLK : (b + 1) * BLK, :], w_ref[...], preferred_element_type=F32
        )
        hidden = hidden.T.astype(BF16)
        hidden_ref[b] = hidden
        wide = hidden.astype(F32)
        source = head_sums(wide * att_src)
        target = head_sums(wide * att_dst)
        target_ref[b] = target
        self_ref[b] = leaky(target + source)


def project(features, weight, att_src, att_dst):
    return pl.pallas_call(
        project_kernel,
        out_shape=(
            jax.ShapeDtypeStruct((NBD, FEAT, BLK), BF16),
            jax.ShapeDtypeStruct((NBD, HEADS, BLK), F32),
            jax.ShapeDtypeStruct((NBD, HEADS, BLK), F32),
            jax.ShapeDtypeStruct((FEAT, BLK), F32),
        ),
        in_specs=[VMEM] * 4,
        out_specs=(VMEM,) * 4,
        compiler_params=params(),
        name="project",
    )(features, weight, att_src.reshape(1, FEAT), att_dst.reshape(1, FEAT))


def mask_kernel(mask_ref, out_ref):
    for n in range(mask_ref.shape[0]):
        for t in range(SLOTS):
            bias = jnp.where(mask_ref[n, t] > 0, 0.0, EMPTY).astype(F32)
            out_ref[n, t] = bias.T


def mask_bias(masks):
    step = 4
    spec = pl.BlockSpec((step, SLOTS, BLK, BLK), lambda i: (i, 0, 0, 0))
    return pl.pallas_call(
        mask_kernel,
        grid=(OWNERS // step,),
        out_shape=jax.ShapeDtypeStruct((OWNERS, SLOTS, BLK, BLK), F32),
        in_specs=[spec],
        out_specs=spec,
        compiler_params=params(),
        cost_estimate=pl.CostEstimate(
            flops=PAIRS * BLK * BLK * 8, bytes_accessed=2 * PAIRS * BLK * BLK * 4, transcendentals=0
        ),
        name="mask_bias",
    )(masks)


def owner_of(scal, k, offset):
    y = lax.rem(scal[PAIRS] + k, NY)
    z = lax.rem(scal[PAIRS + 1] + offset, NZ)
    return y * NZ + z


def halves(values):
    high = values.astype(BF16).astype(F32)
    return high, (values - high).astype(BF16).astype(F32)


def slot_partial(hidden, att, bias, target, out_ref, place):
    sources = head_sums(hidden.astype(F32) * att)
    sources = jnp.concatenate([sources, sources], axis=0).T
    bounds, totals = [], []
    for h in range(HEADS):
        masked = sources[:, h : h + 1] + bias
        top = jnp.max(masked, axis=0, keepdims=True)
        own = target[h : h + 1]
        high, low = halves(leaky(own + top))
        bound = high + low
        weights = jnp.exp2(
            jnp.maximum(masked + (own - bound), 0.2 * masked + (0.2 * own - bound))
        )
        bounds.append((high, low))
        totals.append(halves(jnp.sum(weights, axis=0, keepdims=True)))
        out_ref[place + (pl.ds(h * HEAD, HEAD), slice(None))] = jnp.dot(
            hidden[h * HEAD : (h + 1) * HEAD], weights.astype(BF16), preferred_element_type=F32
        ).astype(BF16)
    rows = [b[0] for b in bounds] + [t[0] for t in totals]
    rows += [b[1] for b in bounds] + [t[1] for t in totals]
    out_ref[place + (pl.ds(FEAT, 16), slice(None))] = jnp.concatenate(rows, axis=0).astype(BF16)


def slots_kernel(offsets, scal, up_mask, down_mask, up_target, down_target, att, *rest):
    pieces, outs = rest[:PIECES], rest[PIECES : PIECES + NY]
    hidden, made, sems = rest[PIECES + NY :]
    step = pl.program_id(0)

    @pl.when(step == 0)
    def _():
        copies = [
            pltpu.make_async_copy(pieces[n], hidden.at[pl.ds(n * NBD, NBD)], sems.at[n])
            for n in range(PIECES)
        ]
        for copy in copies:
            copy.start()
        for copy in copies:
            copy.wait()

    for n, (offset, mask, target) in enumerate(
        zip(offsets, (up_mask, down_mask), (up_target, down_target), strict=True)
    ):
        owner = owner_of(scal, step, offset)
        for t in range(SLOTS):
            pair = scal[owner * SLOTS + t]
            block = lax.rem(pair, SRC_BLOCKS)
            place = lax.div(pair, SRC_BLOCKS)
            holder = lax.div(block, NBD)
            dx = lax.rem(lax.div(holder, NC) - scal[PAIRS + 2] + NX, NX)
            dc = lax.rem(lax.rem(holder, NC) - scal[PAIRS + 3] + NC, NC)
            held = (dx * NC + dc) * NBD + lax.rem(block, NBD)
            slot_partial(hidden[held], att[...], mask[0, t], target[step, place], made, (n, t))

    for k in range(NY):

        @pl.when(step == k)
        def _(k=k):
            outs[k][...] = made[...]


def slots(group, scal, bias, targets, att, pieces):
    offsets = (up_offset(group), down_offset(group))

    def mask_spec(offset):
        return pl.BlockSpec(
            (1, SLOTS, BLK, BLK), lambda i, scal: (owner_of(scal, i, offset), 0, 0, 0)
        )

    def whole(shape):
        return pl.BlockSpec(shape, lambda i, scal: (0,) * len(shape))

    shape = (2, SLOTS, ROWS, BLK)
    return pl.pallas_call(
        functools.partial(slots_kernel, offsets),
        out_shape=(jax.ShapeDtypeStruct(shape, BF16),) * NY,
        grid_spec=pltpu.PrefetchScalarGridSpec(
            num_scalar_prefetch=1,
            grid=(NY,),
            in_specs=[mask_spec(offsets[0]), mask_spec(offsets[1])]
            + [whole((NY, NBD, HEADS, BLK))] * 2
            + [whole((FEAT, BLK))]
            + [ANY] * PIECES,
            out_specs=(whole(shape),) * NY,
            scratch_shapes=[
                pltpu.VMEM((SRC_BLOCKS, FEAT, BLK), BF16),
                pltpu.VMEM(shape, BF16),
                pltpu.SemaphoreType.DMA((PIECES,)),
            ],
        ),
        compiler_params=params(),
        cost_estimate=pl.CostEstimate(
            flops=2 * 16 * BLK * BLK * FEAT, bytes_accessed=8 * 1024 * 1024, transcendentals=16 * HEADS * BLK * BLK
        ),
        name="slots",
    )(scal, bias, bias, targets[offsets[0]], targets[offsets[1]], att, *pieces)


def bound_total(ref, place):
    rows = ref[place + (pl.ds(FEAT, 16), slice(None))].astype(F32)
    both = rows[:8] + rows[8:]
    return both[:HEADS], both[HEADS:]


def merge(slot_list, dense, bounds, totals, sums, self_parts=None):
    for b in range(NBD):
        top = jnp.full((HEADS, BLK), EMPTY, F32)
        if self_parts is not None:
            top = self_parts[0][b]
        for ref in dense:
            top = jnp.maximum(top, bound_total(ref, (b,))[0])
        bounds[b] = top
    for ref, index, place in slot_list:
        bounds[place] = jnp.maximum(bounds[place], bound_total(ref, index)[0])
    for b in range(NBD):
        total = jnp.zeros((HEADS, BLK), F32)
        terms = []
        if self_parts is not None:
            factor = jnp.exp2(self_parts[0][b] - bounds[b])
            total += factor
            terms.append((self_parts[1], (b,), factor))
        for ref in dense:
            bound, more = bound_total(ref, (b,))
            factor = jnp.exp2(bound - bounds[b])
            total += more * factor
            terms.append((ref, (b,), factor))
        totals[b] = total
        for h in range(HEADS):
            rows = pl.ds(h * HEAD, HEAD)
            value = jnp.zeros((HEAD, BLK), F32)
            for ref, index, factor in terms:
                value += ref[index + (rows, slice(None))].astype(F32) * factor[h : h + 1]
            sums[b, rows, :] = value
    for ref, index, place in slot_list:
        bound, more = bound_total(ref, index)
        factor = jnp.exp2(bound - bounds[place])
        totals[place] += more * factor
        for h in range(HEADS):
            rows = pl.ds(h * HEAD, HEAD)
            sums[place, rows, :] += (
                ref[index + (rows, slice(None))].astype(F32) * factor[h : h + 1]
            )


def placed(scals, offset, refs, n):
    owner = owner_of(scals[0], 0, offset)
    return [
        (refs[k], (n, t), lax.div(scals[k][owner * SLOTS + t], SRC_BLOCKS))
        for k in range(NY)
        for t in range(SLOTS)
    ]


def write_dense(out, bounds, totals, sums):
    for b in range(NBD):
        out[b, pl.ds(0, FEAT), :] = sums[b].astype(BF16)
        both = halves(jnp.concatenate([bounds[b], totals[b]], axis=0))
        out[b, pl.ds(FEAT, 16), :] = jnp.concatenate(both, axis=0).astype(BF16)


def merge_kernel(work, *refs):
    scals, refs = refs[:NY], refs[NY:]
    parts, refs = refs[:NY], refs[NY:]
    n_dense = sum(w[2] for w in work)
    dense, refs = refs[:n_dense], refs[n_dense:]
    outs, (bounds, totals, sums) = refs[: len(work)], refs[len(work) :]
    for out, (offset, n, count) in zip(outs, work, strict=True):
        mine, dense = dense[:count], dense[count:]
        merge(placed(scals, offset, parts, n), mine, bounds, totals, sums)
        write_dense(out, bounds, totals, sums)


def merge_scratch():
    return [
        pltpu.VMEM((NBD, HEADS, BLK), F32),
        pltpu.VMEM((NBD, HEADS, BLK), F32),
        pltpu.VMEM((NBD, FEAT, BLK), F32),
    ]


SMEM = pl.BlockSpec(memory_space=pltpu.SMEM)


def merge_group(work, scals, parts, dense):
    return pl.pallas_call(
        functools.partial(merge_kernel, work),
        out_shape=(jax.ShapeDtypeStruct((NBD, ROWS, BLK), BF16),) * len(work),
        in_specs=[SMEM] * NY + [VMEM] * (NY + len(dense)),
        out_specs=(VMEM,) * len(work),
        scratch_shapes=merge_scratch(),
        compiler_params=params(),
        cost_estimate=pl.CostEstimate(flops=20_000_000, bytes_accessed=2_000_000, transcendentals=0),
        name="merge",
    )(*scals, *parts, *dense)


def final_kernel(work, *refs):
    scals, refs = refs[:NY], refs[NY:]
    parts, refs = refs[:NY], refs[NY:]
    dense, (self_ref, hidden_ref, bias_ref, out, bounds, totals, sums) = refs[:2], refs[2:]
    offset, n = work
    merge(placed(scals, offset, parts, n), dense, bounds, totals, sums, (self_ref, hidden_ref))
    for b in range(NBD):
        scale = 1.0 / totals[b]
        value = jnp.concatenate(
            [sums[b, pl.ds(h * HEAD, HEAD), :] * scale[h : h + 1] for h in range(HEADS)], axis=0
        )
        value = value.T + bias_ref[...]
        out[pl.ds(b * BLK, BLK), :] = jnp.where(
            value > 0, value, jnp.exp(jnp.minimum(value, 0.0)) - 1.0
        )


def finish(work, scals, parts, dense, self_logit, hidden, bias):
    return pl.pallas_call(
        functools.partial(final_kernel, work),
        out_shape=jax.ShapeDtypeStruct((NBD * BLK, FEAT), F32),
        in_specs=[SMEM] * NY + [VMEM] * (NY + 5),
        out_specs=VMEM,
        scratch_shapes=merge_scratch(),
        compiler_params=params(),
        name="finish",
    )(*scals, *parts, *dense, self_logit, hidden, bias.reshape(1, FEAT))


def body(features, weight, att_src, att_dst, bias, block_pairs, edge_masks):
    src = lax.axis_index("src")
    dst = lax.axis_index("dst")
    place = jnp.stack([src // NZ, src % NZ, dst // NC, dst % NC]).astype(jnp.int32)
    scal = jnp.concatenate([block_pairs.reshape(-1), place])
    scals = [scal] + [lax.ppermute(scal, "src", y_from(-k)) for k in range(1, NY)]

    hidden, own_target, self_logit, att = project(features, weight, att_src, att_dst)
    along_x = [hidden] + [lax.ppermute(hidden, "dst", x_from(k)) for k in range(1, NX)]
    pieces = []
    for piece in along_x:
        pieces += [piece, lax.ppermute(piece, "dst", core_from(1))]
    along_y = jnp.stack(
        [own_target] + [lax.ppermute(own_target, "src", y_from(k)) for k in range(1, NY)]
    )
    targets = [along_y] + [lax.ppermute(along_y, "src", z_from(k)) for k in range(1, NZ)]

    masks = mask_bias(edge_masks.reshape(OWNERS, SLOTS, BLK, BLK))

    up, down = [], []
    for group in range(GROUPS):
        made = slots(group, scal, masks, targets, att, pieces)
        parts = [made[0]] + [lax.ppermute(made[k], "src", y_from(-k)) for k in range(1, NY)]
        work = [(up_offset(group), 0, len(up))]
        if group < GROUPS - 1:
            work.append((down_offset(group), 1, len(down)))
            sent = merge_group(work, scals, parts, up + down)
            down = [lax.ppermute(sent[1], "src", z_from(1))]
        else:
            sent = merge_group(work, scals, parts, up)
        up = [lax.ppermute(sent[0], "src", z_from(-1))]
    return finish((0, 1), scals, parts, up + down, self_logit, hidden, bias)


def solution(mesh):
    placed_at = (
        P(("dst", "src"), None),
        P(),
        P(),
        P(),
        P(),
        P("src", "dst", None, None),
        P("src", "dst", None, None, None, None),
    )
    return jax.shard_map(
        body, mesh=mesh, in_specs=placed_at, out_specs=P(("dst", "src"), None), check_vma=False
    )
```

```python
import functools

import jax
import jax.numpy as jnp
from jax import lax
from jax.experimental import pallas as pl
from jax.experimental.pallas import tpu as pltpu
from jax.sharding import PartitionSpec as P

HEADS = 4
HEAD = 64
FEAT = HEADS * HEAD
BLK = 128
NBD = 4
SLOTS = 2
NY, NZ, NX, NC = 4, 8, 4, 2
LOG_NZ = 3
PIECES = NX * NC
SRC_BLOCKS = NBD * PIECES
OWNERS = NY * NZ
PAIRS = OWNERS * SLOTS
ROWS = FEAT + 16
GATE_COST = 800_000_000
LOG2E = 1.4426950408889634
EMPTY = -(2.0**100)
F32 = jnp.float32
BF16 = jnp.bfloat16
VMEM = pl.BlockSpec(memory_space=pltpu.VMEM)
ANY = pl.BlockSpec(memory_space=pl.ANY)


def params(**more):
    return pltpu.CompilerParams(vmem_limit_bytes=48 * 1024 * 1024, **more)


def leaky(values):
    return jnp.maximum(values, 0.2 * values)


def y_from(k):
    return [(y * NZ + z, (y - k) % NY * NZ + z) for y in range(NY) for z in range(NZ)]


def z_from(k):
    return [(y * NZ + z, y * NZ + (z - k) % NZ) for y in range(NY) for z in range(NZ)]


def x_from(k):
    return [(x * NC + c, (x - k) % NX * NC + c) for x in range(NX) for c in range(NC)]


def core_from(k):
    return [(x * NC + c, x * NC + (c - k) % NC) for x in range(NX) for c in range(NC)]


PLAN = ((4,), (3, -3), (2, -2), (1, -1), (0,))


def head_sums(products):
    return jnp.concatenate(
        [jnp.sum(products[h * HEAD : (h + 1) * HEAD], axis=0, keepdims=True) for h in range(HEADS)],
        axis=0,
    )


def prepare_kernel(x_ref, src_hbm, dst_hbm, hidden_ref, target_ref, self_ref, att_ref, src_ref, dst_ref, sems):
    copies = [
        pltpu.make_async_copy(src_hbm, src_ref, sems.at[0]),
        pltpu.make_async_copy(dst_hbm, dst_ref, sems.at[1]),
    ]
    for copy in copies:
        copy.start()
    for copy in copies:
        copy.wait()
    att_src = jnp.broadcast_to(src_ref[...] * LOG2E, (BLK, FEAT)).T
    att_dst = jnp.broadcast_to(dst_ref[...] * LOG2E, (BLK, FEAT)).T
    att_ref[...] = att_src
    for b in range(NBD):
        wide = x_ref[b * BLK : (b + 1) * BLK, :].astype(F32).T
        hidden_ref[b] = wide.astype(BF16)
        source = head_sums(wide * att_src)
        target = head_sums(wide * att_dst)
        target_ref[b] = target
        self_ref[b] = leaky(target + source)


def prepare(hidden, att_src, att_dst):
    return pl.pallas_call(
        prepare_kernel,
        out_shape=(
            jax.ShapeDtypeStruct((NBD, FEAT, BLK), BF16),
            jax.ShapeDtypeStruct((NBD, HEADS, BLK), F32),
            jax.ShapeDtypeStruct((NBD, HEADS, BLK), F32),
            jax.ShapeDtypeStruct((FEAT, BLK), F32),
        ),
        in_specs=[VMEM, ANY, ANY],
        out_specs=(VMEM,) * 4,
        scratch_shapes=[
            pltpu.VMEM((1, FEAT), F32),
            pltpu.VMEM((1, FEAT), F32),
            pltpu.SemaphoreType.DMA((2,)),
        ],
        compiler_params=params(),
        name="prepare",
    )(hidden, att_src.reshape(1, FEAT), att_dst.reshape(1, FEAT))


def gate_kernel(*refs):
    refs[-1][...] = jnp.zeros((8, BLK), F32)


def gate(pieces):
    return pl.pallas_call(
        gate_kernel,
        out_shape=jax.ShapeDtypeStruct((8, BLK), F32),
        in_specs=[ANY] * PIECES,
        out_specs=VMEM,
        compiler_params=params(),
        cost_estimate=pl.CostEstimate(flops=GATE_COST, bytes_accessed=1000, transcendentals=0),
        name="gate",
    )(*pieces)


def owner_of(scal, k, offset):
    src = scal[PAIRS]
    return ((((src >> LOG_NZ) + k) & (NY - 1)) << LOG_NZ) | ((src + offset) & (NZ - 1))


def halves(values):
    high = values.astype(BF16).astype(F32)
    return high, (values - high).astype(BF16).astype(F32)


def slot_partial(hidden, att, bias, target, out_ref, place):
    sources = head_sums(hidden.astype(F32) * att)
    sources = jnp.concatenate([sources, sources], axis=0).T
    bounds, totals = [], []
    for h in range(HEADS):
        masked = sources[:, h : h + 1] + bias
        top = jnp.max(masked, axis=0, keepdims=True)
        own = target[h : h + 1]
        high, low = halves(leaky(own + top))
        bound = high + low
        weights = jnp.exp2(
            jnp.maximum(masked + (own - bound), 0.2 * masked + (0.2 * own - bound))
        )
        bounds.append((high, low))
        totals.append(halves(jnp.sum(weights, axis=0, keepdims=True)))
        out_ref[place + (pl.ds(h * HEAD, HEAD), slice(None))] = jnp.dot(
            hidden[h * HEAD : (h + 1) * HEAD], weights.astype(BF16), preferred_element_type=F32
        ).astype(BF16)
    rows = [b[0] for b in bounds] + [t[0] for t in totals]
    rows += [b[1] for b in bounds] + [t[1] for t in totals]
    out_ref[place + (pl.ds(FEAT, 16), slice(None))] = jnp.concatenate(rows, axis=0).astype(BF16)


def slots_kernel(offsets, first, scal, token, targets, att, *rest):
    del token
    n_own, n_in = len(offsets), PIECES if first else 1
    masks, sources, rest = rest[:n_own], rest[n_own : n_own + n_in], rest[n_own + n_in :]
    step = pl.program_id(0)
    if first:
        *outs, hidden, made, sems = rest

        @pl.when(step == 0)
        def _():
            copies = [
                pltpu.make_async_copy(sources[n], hidden.at[pl.ds(n * NBD, NBD)], sems.at[n])
                for n in range(PIECES)
            ]
            for copy in copies:
                copy.start()
            for copy in copies:
                copy.wait()

    else:
        (hidden,), (*outs, made) = sources, rest
    for n, (offset, mask) in enumerate(zip(offsets, masks, strict=True)):
        owner = owner_of(scal, step, offset)
        for t in range(SLOTS):
            pair = scal[owner * SLOTS + t]
            block = pair & (SRC_BLOCKS - 1)
            place = pair >> (SRC_BLOCKS.bit_length() - 1)
            holder = block >> (NBD.bit_length() - 1)
            dst = scal[PAIRS + 1]
            dx = ((holder >> 1) - (dst >> 1)) & (NX - 1)
            dc = (holder ^ dst) & (NC - 1)
            held = ((dx * NC + dc) * NBD) | (block & (NBD - 1))
            bias = jnp.where(mask[0, t] > 0, 0.0, EMPTY).astype(F32).T
            slot_partial(hidden[held], att[...], bias, targets[owner, place], made, (n, t))

    for k in range(NY):

        @pl.when(step == k)
        def _(k=k):
            outs[k][...] = made[...]


def slots(offsets, scal, token, masks, targets, att, source):
    first = isinstance(source, list)

    def mask_spec(offset):
        return pl.BlockSpec(
            (1, SLOTS, BLK, BLK), lambda i, scal: (owner_of(scal, i, offset), 0, 0, 0)
        )

    shape = (len(offsets), SLOTS, ROWS, BLK)
    out_shape = (jax.ShapeDtypeStruct(shape, BF16),) * NY
    scratch = [pltpu.VMEM(shape, BF16)]
    if first:
        out_shape += (jax.ShapeDtypeStruct((SRC_BLOCKS, FEAT, BLK), BF16),)
        scratch.append(pltpu.SemaphoreType.DMA((PIECES,)))
    return pl.pallas_call(
        functools.partial(slots_kernel, offsets, first),
        out_shape=out_shape,
        grid_spec=pltpu.PrefetchScalarGridSpec(
            num_scalar_prefetch=1,
            grid=(NY,),
            in_specs=[ANY, VMEM, VMEM]
            + [mask_spec(offset) for offset in offsets]
            + ([ANY] * PIECES if first else [VMEM]),
            out_specs=(VMEM,) * len(out_shape),
            scratch_shapes=scratch,
        ),
        compiler_params=params(),
        cost_estimate=pl.CostEstimate(flops=1000, bytes_accessed=1000, transcendentals=0),
        name="slots",
    )(scal, token, targets, att, *[masks] * len(offsets), *(source if first else [source]))


def bound_total(ref, place):
    rows = ref[place + (pl.ds(FEAT, 16), slice(None))].astype(F32)
    both = rows[:8] + rows[8:]
    return both[:HEADS], both[HEADS:]


def merge(slot_list, dense, bounds, totals, sums, given=None):
    for b in range(NBD):
        top = jnp.full((HEADS, BLK), EMPTY, F32) if given is None else given[0][b]
        for ref in dense:
            top = jnp.maximum(top, bound_total(ref, (b,))[0])
        bounds[b] = top
    for ref, index, place in slot_list:
        bounds[place] = jnp.maximum(bounds[place], bound_total(ref, index)[0])
    for b in range(NBD):
        total = jnp.zeros((HEADS, BLK), F32)
        terms = []
        if given is not None:
            factor = jnp.exp2(given[0][b] - bounds[b])
            total += factor if given[1] is None else given[1][b] * factor
            terms.append((given[2], (b,), factor))
        for ref in dense:
            bound, more = bound_total(ref, (b,))
            factor = jnp.exp2(bound - bounds[b])
            total += more * factor
            terms.append((ref, (b,), factor))
        totals[b] = total
        for h in range(HEADS):
            rows = pl.ds(h * HEAD, HEAD)
            value = jnp.zeros((HEAD, BLK), F32)
            for ref, index, factor in terms:
                value += ref[index + (rows, slice(None))].astype(F32) * factor[h : h + 1]
            sums[b, rows, :] = value
    for ref, index, place in slot_list:
        bound, more = bound_total(ref, index)
        factor = jnp.exp2(bound - bounds[place])
        totals[place] += more * factor
        for h in range(HEADS):
            rows = pl.ds(h * HEAD, HEAD)
            sums[place, rows, :] += (
                ref[index + (rows, slice(None))].astype(F32) * factor[h : h + 1]
            )


def placed(scal, every_pair, offset, refs, n):
    owner = owner_of(scal, 0, offset)
    found = []
    for k in range(NY):
        for t in range(SLOTS):
            place = every_pair[k, owner * SLOTS + t] >> (SRC_BLOCKS.bit_length() - 1)
            found.append((refs[k], (n, t), place))
    return found


def write_dense(out, bounds, totals, sums):
    for b in range(NBD):
        out[b, pl.ds(0, FEAT), :] = sums[b].astype(BF16)
        both = halves(jnp.concatenate([bounds[b], totals[b]], axis=0))
        out[b, pl.ds(FEAT, 16), :] = jnp.concatenate(both, axis=0).astype(BF16)


def merge_kernel(work, scal, every_pair, *refs):
    parts, refs = refs[:NY], refs[NY:]
    n_dense = sum(w[1] for w in work)
    dense, refs = refs[:n_dense], refs[n_dense:]
    outs, (bounds, totals, sums) = refs[: len(work)], refs[len(work) :]
    for n, (out, (offset, count)) in enumerate(zip(outs, work, strict=True)):
        mine, dense = dense[:count], dense[count:]
        merge(placed(scal, every_pair, offset, parts, n), mine, bounds, totals, sums)
        write_dense(out, bounds, totals, sums)


SUMS = ((NBD, HEADS, BLK), (NBD, HEADS, BLK), (NBD, FEAT, BLK))
SMEM = pl.BlockSpec(memory_space=pltpu.SMEM)


def merge_group(work, scal, every_pair, parts, dense):
    return pl.pallas_call(
        functools.partial(merge_kernel, work),
        out_shape=(jax.ShapeDtypeStruct((NBD, ROWS, BLK), BF16),) * len(work),
        in_specs=[SMEM] * 2 + [VMEM] * (NY + len(dense)),
        out_specs=(VMEM,) * len(work),
        scratch_shapes=[pltpu.VMEM(shape, F32) for shape in SUMS],
        compiler_params=params(),
        cost_estimate=pl.CostEstimate(flops=1000, bytes_accessed=1000, transcendentals=0),
        name="merge",
    )(scal, every_pair, *parts, *dense)


def home_kernel(scal, every_pair, *refs):
    parts, (self_ref, hidden_ref, bounds, totals, sums) = refs[:NY], refs[NY:]
    found = placed(scal, every_pair, 0, parts, 0)
    merge(found, (), bounds, totals, sums, (self_ref, None, hidden_ref))


def merge_home(scal, every_pair, parts, self_logit, hidden):
    return pl.pallas_call(
        home_kernel,
        out_shape=tuple(jax.ShapeDtypeStruct(shape, F32) for shape in SUMS),
        in_specs=[SMEM] * 2 + [VMEM] * (NY + 2),
        out_specs=(VMEM,) * 3,
        compiler_params=params(),
        cost_estimate=pl.CostEstimate(flops=1000, bytes_accessed=1000, transcendentals=0),
        name="merge_home",
    )(scal, every_pair, *parts, self_logit, hidden)


def finish_kernel(up, down, home_bounds, home_totals, home_sums, bias_ref, out, bounds, totals, sums):
    merge((), (up, down), bounds, totals, sums, (home_bounds, home_totals, home_sums))
    for b in range(NBD):
        scale = 1.0 / totals[b]
        value = jnp.concatenate(
            [sums[b, pl.ds(h * HEAD, HEAD), :] * scale[h : h + 1] for h in range(HEADS)], axis=0
        )
        value = value.T + bias_ref[...]
        out[pl.ds(b * BLK, BLK), :] = jnp.where(
            value > 0, value, jnp.exp(jnp.minimum(value, 0.0)) - 1.0
        )


def finish(up, down, home, bias):
    return pl.pallas_call(
        finish_kernel,
        out_shape=jax.ShapeDtypeStruct((NBD * BLK, FEAT), F32),
        in_specs=[VMEM] * 6,
        out_specs=VMEM,
        scratch_shapes=[pltpu.VMEM(shape, F32) for shape in SUMS],
        compiler_params=params(),
        name="finish",
    )(up, down, *home, bias.reshape(1, FEAT))


def body(features, weight, att_src, att_dst, bias, block_pairs, edge_masks):
    masks = edge_masks.reshape(OWNERS, SLOTS, BLK, BLK)
    hidden = jnp.dot(features, weight, preferred_element_type=F32).astype(BF16)
    hidden, own_target, self_logit, att = prepare(hidden, att_src, att_dst)
    along_x = [hidden] + [lax.ppermute(hidden, "dst", x_from(k)) for k in range(1, NX)]

    src = lax.axis_index("src")
    dst = lax.axis_index("dst")
    pairs = block_pairs.reshape(-1)
    scal = jnp.concatenate([pairs, jnp.stack([src, dst]).astype(jnp.int32)])

    told = jnp.broadcast_to(own_target[None], (OWNERS,) + own_target.shape)
    told = lax.all_to_all(told, "src", 0, 0)

    pieces = []
    for piece in along_x:
        pieces += [piece, lax.ppermute(piece, "dst", core_from(1))]
    pairs, pieces[-1] = lax.optimization_barrier((pairs, pieces[-1]))
    every_pair = jnp.stack([pairs] + [lax.ppermute(pairs, "src", y_from(-k)) for k in range(1, NY)])
    token = gate(pieces)
    scal, every_pair = lax.optimization_barrier((scal, every_pair))

    up, down = (), ()
    made, parts = [], []
    source = pieces
    for step, offsets in enumerate(PLAN):
        made.append(slots(offsets, scal, token, masks, told, att, source))
        if step == 0:
            source = made[0][NY]
        parts.append(
            [made[-1][0]] + [lax.ppermute(made[-1][k], "src", y_from(-k)) for k in range(1, NY)]
        )
    for step, offsets in enumerate(PLAN[:-1]):
        work = [(offsets[0], len(up))] + [(offset, len(down)) for offset in offsets[1:]]
        if step == len(PLAN) - 2:
            parts[step][0], parts[step + 1][1] = lax.optimization_barrier(
                (parts[step][0], parts[step + 1][1])
            )
        sent = merge_group(work, scal, every_pair, parts[step], up + down)
        up = (lax.ppermute(sent[0], "src", z_from(-1)),)
        if len(sent) > 1:
            down = (lax.ppermute(sent[1], "src", z_from(1)),)
    home = merge_home(scal, every_pair, parts[-1], self_logit, hidden)
    return finish(up[0], down[0], home, bias)


def solution(mesh):
    placed_at = (
        P(("dst", "src"), None),
        P(),
        P(),
        P(),
        P(),
        P("src", "dst", None, None),
        P("src", "dst", None, None, None, None),
    )
    return jax.shard_map(
        body, mesh=mesh, in_specs=placed_at, out_specs=P(("dst", "src"), None), check_vma=False
    )
```

```python
import functools

import jax
import jax.numpy as jnp
from jax import lax
from jax.experimental import pallas as pl
from jax.experimental.pallas import tpu as pltpu
from jax.sharding import PartitionSpec as P

HEADS = 4
HEAD = 64
FEAT = HEADS * HEAD
BLK = 128
NBD = 4
SLOTS = 2
NY, NZ, NX, NC = 4, 8, 4, 2
LOG_NZ = 3
PIECES = NX * NC
SRC_BLOCKS = NBD * PIECES
OWNERS = NY * NZ
PAIRS = OWNERS * SLOTS
ROWS = FEAT + 16
GATE_COST = 1400_000_000
LOG2E = 1.4426950408889634
EMPTY = -(2.0**100)
F32 = jnp.float32
BF16 = jnp.bfloat16
VMEM = pl.BlockSpec(memory_space=pltpu.VMEM)
ANY = pl.BlockSpec(memory_space=pl.ANY)


def params(**more):
    return pltpu.CompilerParams(vmem_limit_bytes=46 * 1024 * 1024, **more)


def leaky(values):
    return jnp.maximum(values, 0.2 * values)


def y_from(k):
    return [(y * NZ + z, (y - k) % NY * NZ + z) for y in range(NY) for z in range(NZ)]


def z_from(k):
    return [(y * NZ + z, y * NZ + (z - k) % NZ) for y in range(NY) for z in range(NZ)]


def x_from(k):
    return [(x * NC + c, (x - k) % NX * NC + c) for x in range(NX) for c in range(NC)]


def core_from(k):
    return [(x * NC + c, x * NC + (c - k) % NC) for x in range(NX) for c in range(NC)]


PLAN = ((4,), (3, -3), (2, -2), (1, -1, 0))
NEXT = {4: 3, 3: 2, 2: 1, 1: 0, -3: -2, -2: -1, -1: 0}


def head_sums(products):
    return jnp.concatenate(
        [jnp.sum(products[h * HEAD : (h + 1) * HEAD], axis=0, keepdims=True) for h in range(HEADS)],
        axis=0,
    )


def prepare_kernel(x_ref, both_ref, hidden_ref, target_ref, self_ref, att_ref):
    att_src = jnp.broadcast_to(both_ref[0:1] * LOG2E, (BLK, FEAT)).T
    att_dst = jnp.broadcast_to(both_ref[1:2] * LOG2E, (BLK, FEAT)).T
    att_ref[...] = att_src
    for b in range(NBD):
        wide = x_ref[b * BLK : (b + 1) * BLK, :].astype(F32).T
        hidden_ref[b] = wide.astype(BF16)
        source = head_sums(wide * att_src)
        target = head_sums(wide * att_dst)
        target_ref[b] = target
        self_ref[b] = leaky(target + source)


def prepare(hidden, att_src, att_dst):
    return pl.pallas_call(
        prepare_kernel,
        out_shape=(
            jax.ShapeDtypeStruct((NBD, FEAT, BLK), BF16),
            jax.ShapeDtypeStruct((NBD, HEADS, BLK), F32),
            jax.ShapeDtypeStruct((NBD, HEADS, BLK), F32),
            jax.ShapeDtypeStruct((FEAT, BLK), F32),
        ),
        in_specs=[VMEM] * 2,
        out_specs=(VMEM,) * 4,
        compiler_params=params(),
        name="prepare",
    )(hidden, jnp.stack([att_src, att_dst]))


def gate_kernel(*refs):
    refs[-1][...] = jnp.zeros((8, BLK), F32)


def gate(*arrays):
    return pl.pallas_call(
        gate_kernel,
        out_shape=jax.ShapeDtypeStruct((8, BLK), F32),
        in_specs=[ANY] * len(arrays),
        out_specs=VMEM,
        compiler_params=params(),
        cost_estimate=pl.CostEstimate(flops=GATE_COST, bytes_accessed=1000, transcendentals=0),
        name="gate",
    )(*arrays)


def mask_kernel(mask_ref, out_ref):
    for n in range(mask_ref.shape[0]):
        for t in range(SLOTS):
            bias = jnp.where(mask_ref[n, t] > 0, 0.0, EMPTY).astype(F32)
            out_ref[n, t] = bias.T.astype(BF16)


def mask_bias(masks):
    step = 4
    spec = pl.BlockSpec((step, SLOTS, BLK, BLK), lambda i: (i, 0, 0, 0))
    return pl.pallas_call(
        mask_kernel,
        grid=(OWNERS // step,),
        out_shape=jax.ShapeDtypeStruct((OWNERS, SLOTS, BLK, BLK), BF16),
        in_specs=[spec],
        out_specs=spec,
        compiler_params=params(),
        cost_estimate=pl.CostEstimate(
            flops=PAIRS * BLK * BLK * 8, bytes_accessed=PAIRS * BLK * BLK * 6, transcendentals=0
        ),
        name="mask_bias",
    )(masks)


def owner_of(scal, k, offset):
    src = scal[PAIRS]
    return ((((src >> LOG_NZ) + k) & (NY - 1)) << LOG_NZ) | ((src + offset) & (NZ - 1))


def halves(values):
    high = values.astype(BF16).astype(F32)
    return high, (values - high).astype(BF16).astype(F32)


def slot_partial(hidden, att, bias, target, out_ref, place):
    sources = head_sums(hidden.astype(F32) * att)
    sources = jnp.concatenate([sources, sources], axis=0).T
    bounds, totals = [], []
    for h in range(HEADS):
        masked = sources[:, h : h + 1] + bias
        top = jnp.max(masked, axis=0, keepdims=True)
        own = target[h : h + 1]
        high, low = halves(leaky(own + top))
        bound = high + low
        weights = jnp.exp2(
            jnp.maximum(masked + (own - bound), 0.2 * masked + (0.2 * own - bound))
        )
        bounds.append((high, low))
        totals.append(halves(jnp.sum(weights, axis=0, keepdims=True)))
        out_ref[place + (pl.ds(h * HEAD, HEAD), slice(None))] = jnp.dot(
            hidden[h * HEAD : (h + 1) * HEAD], weights.astype(BF16), preferred_element_type=F32
        ).astype(BF16)
    rows = [b[0] for b in bounds] + [t[0] for t in totals]
    rows += [b[1] for b in bounds] + [t[1] for t in totals]
    out_ref[place + (pl.ds(FEAT, 16), slice(None))] = jnp.concatenate(rows, axis=0).astype(BF16)


def slots_kernel(offsets, first, scal, token, targets, att, bias, *rest):
    del token
    if first:
        sources, (*outs, hidden, made, sems) = rest[:PIECES], rest[PIECES:]
        copies = [
            pltpu.make_async_copy(sources[n], hidden.at[pl.ds(n * NBD, NBD)], sems.at[n])
            for n in range(PIECES)
        ]
        for copy in copies:
            copy.start()
        for copy in copies:
            copy.wait()
    else:
        hidden, *outs, made = rest
    dst = scal[PAIRS + 1]
    together = made.shape[0]

    def some(step, carry):
        for part in range(together):
            for n, offset in enumerate(offsets):
                owner = owner_of(scal, step * together + part, offset)
                for t in range(SLOTS):
                    pair = scal[owner * SLOTS + t]
                    block = pair & (SRC_BLOCKS - 1)
                    place = pair >> (SRC_BLOCKS.bit_length() - 1)
                    holder = block >> (NBD.bit_length() - 1)
                    dx = ((holder >> 1) - (dst >> 1)) & (NX - 1)
                    dc = (holder ^ dst) & (NC - 1)
                    held = ((dx * NC + dc) * NBD) | (block & (NBD - 1))
                    slot_partial(
                        hidden[held], att[...], bias[owner, t].astype(F32), targets[owner, place], made, (part, n, t)
                    )
        for other in range(NY // together):

            @pl.when(step == other)
            def _(other=other):
                for part in range(together):
                    outs[other * together + part][...] = made[part]

        return carry

    lax.fori_loop(0, NY // together, some, 0)


def slots(offsets, scal, token, bias, targets, att, source):
    first = isinstance(source, list)
    shape = (len(offsets), SLOTS, ROWS, BLK)
    out_shape = (jax.ShapeDtypeStruct(shape, BF16),) * NY
    scratch = [pltpu.VMEM((max(1, 2 // len(offsets)),) + shape, BF16)]
    if first:
        out_shape += (jax.ShapeDtypeStruct((SRC_BLOCKS, FEAT, BLK), BF16),)
        scratch.append(pltpu.SemaphoreType.DMA((PIECES,)))
    return pl.pallas_call(
        functools.partial(slots_kernel, offsets, first),
        out_shape=out_shape,
        in_specs=[SMEM, ANY, VMEM, VMEM, VMEM] + ([ANY] * PIECES if first else [VMEM]),
        out_specs=(VMEM,) * len(out_shape),
        scratch_shapes=scratch,
        compiler_params=params(),
        cost_estimate=pl.CostEstimate(flops=1000, bytes_accessed=1000, transcendentals=0),
        name="slots",
    )(scal, token, targets, att, bias, *(source if first else [source]))


def bound_total(ref, place):
    rows = ref[place + (pl.ds(FEAT, 16), slice(None))].astype(F32)
    both = rows[:8] + rows[8:]
    return both[:HEADS], both[HEADS:]


def merge(slot_list, dense, bounds, totals, sums, given=None):
    for b in range(NBD):
        top = jnp.full((HEADS, BLK), EMPTY, F32) if given is None else given[0][b]
        for ref in dense:
            top = jnp.maximum(top, bound_total(ref, (b,))[0])
        bounds[b] = top
    for ref, index, place in slot_list:
        bounds[place] = jnp.maximum(bounds[place], bound_total(ref, index)[0])
    for b in range(NBD):
        total = jnp.zeros((HEADS, BLK), F32)
        terms = []
        if given is not None:
            factor = jnp.exp2(given[0][b] - bounds[b])
            total += factor if given[1] is None else given[1][b] * factor
            terms.append((given[2], (b,), factor))
        for ref in dense:
            bound, more = bound_total(ref, (b,))
            factor = jnp.exp2(bound - bounds[b])
            total += more * factor
            terms.append((ref, (b,), factor))
        totals[b] = total
        for h in range(HEADS):
            rows = pl.ds(h * HEAD, HEAD)
            value = jnp.zeros((HEAD, BLK), F32)
            for ref, index, factor in terms:
                value += ref[index + (rows, slice(None))].astype(F32) * factor[h : h + 1]
            sums[b, rows, :] = value
    for ref, index, place in slot_list:
        bound, more = bound_total(ref, index)
        factor = jnp.exp2(bound - bounds[place])
        totals[place] += more * factor
        for h in range(HEADS):
            rows = pl.ds(h * HEAD, HEAD)
            sums[place, rows, :] += (
                ref[index + (rows, slice(None))].astype(F32) * factor[h : h + 1]
            )


def placed(scal, every_pair, offset, refs, n):
    owner = owner_of(scal, 0, offset)
    found = []
    for k in range(NY):
        maker = owner_of(scal, -k, 0)
        for t in range(SLOTS):
            place = every_pair[maker * SLOTS + t, owner] >> (SRC_BLOCKS.bit_length() - 1)
            found.append((refs[k], (n, t), place))
    return found


def write_dense(out, bounds, totals, sums):
    for b in range(NBD):
        out[b, pl.ds(0, FEAT), :] = sums[b].astype(BF16)
        both = halves(jnp.concatenate([bounds[b], totals[b]], axis=0))
        out[b, pl.ds(FEAT, 16), :] = jnp.concatenate(both, axis=0).astype(BF16)


def merge_kernel(work, scal, every_pair, *refs):
    parts, refs = refs[:NY], refs[NY:]
    n_dense = sum(w[1] for w in work)
    dense, refs = refs[:n_dense], refs[n_dense:]
    outs, (bounds, totals, sums) = refs[: len(work)], refs[len(work) :]
    for n, (out, (offset, count)) in enumerate(zip(outs, work, strict=True)):
        mine, dense = dense[:count], dense[count:]
        merge(placed(scal, every_pair, offset, parts, n), mine, bounds, totals, sums)
        write_dense(out, bounds, totals, sums)


SUMS = ((NBD, HEADS, BLK), (NBD, HEADS, BLK), (NBD, FEAT, BLK))
SMEM = pl.BlockSpec(memory_space=pltpu.SMEM)


def merge_group(work, scal, every_pair, parts, dense):
    return pl.pallas_call(
        functools.partial(merge_kernel, work),
        out_shape=(jax.ShapeDtypeStruct((NBD, ROWS, BLK), BF16),) * len(work),
        in_specs=[SMEM] * 2 + [VMEM] * (NY + len(dense)),
        out_specs=(VMEM,) * len(work),
        scratch_shapes=[pltpu.VMEM(shape, F32) for shape in SUMS],
        compiler_params=params(),
        cost_estimate=pl.CostEstimate(flops=1000, bytes_accessed=1000, transcendentals=0),
        name="merge",
    )(scal, every_pair, *parts, *dense)


def home_kernel(n, scal, every_pair, *refs):
    parts, (self_ref, hidden_ref, bounds, totals, sums) = refs[:NY], refs[NY:]
    found = placed(scal, every_pair, 0, parts, n)
    merge(found, (), bounds, totals, sums, (self_ref, None, hidden_ref))


def merge_home(scal, every_pair, parts, self_logit, hidden):
    return pl.pallas_call(
        functools.partial(home_kernel, PLAN[-1].index(0)),
        out_shape=tuple(jax.ShapeDtypeStruct(shape, F32) for shape in SUMS),
        in_specs=[SMEM] * 2 + [VMEM] * (NY + 2),
        out_specs=(VMEM,) * 3,
        compiler_params=params(),
        cost_estimate=pl.CostEstimate(flops=1000, bytes_accessed=1000, transcendentals=0),
        name="merge_home",
    )(scal, every_pair, *parts, self_logit, hidden)


def finish_kernel(*refs):
    dense, refs = refs[:-8], refs[-8:]
    home_bounds, home_totals, home_sums, bias_ref, out, bounds, totals, sums = refs
    merge((), dense, bounds, totals, sums, (home_bounds, home_totals, home_sums))
    for b in range(NBD):
        scale = 1.0 / totals[b]
        value = jnp.concatenate(
            [sums[b, pl.ds(h * HEAD, HEAD), :] * scale[h : h + 1] for h in range(HEADS)], axis=0
        )
        value = value.T + bias_ref[...]
        out[pl.ds(b * BLK, BLK), :] = jnp.where(
            value > 0, value, jnp.exp(jnp.minimum(value, 0.0)) - 1.0
        )


def finish(dense, home, bias):
    return pl.pallas_call(
        finish_kernel,
        out_shape=jax.ShapeDtypeStruct((NBD * BLK, FEAT), F32),
        in_specs=[VMEM] * (len(dense) + 4),
        out_specs=VMEM,
        scratch_shapes=[pltpu.VMEM(shape, F32) for shape in SUMS],
        compiler_params=params(),
        name="finish",
    )(*dense, *home, bias.reshape(1, FEAT))


def body(features, weight, att_src, att_dst, bias, block_pairs, edge_masks):
    masks = edge_masks.reshape(OWNERS, SLOTS, BLK, BLK)
    hidden = jnp.dot(features, weight, preferred_element_type=F32).astype(BF16)
    hidden, own_target, self_logit, att = prepare(hidden, att_src, att_dst)
    along_x = [hidden] + [lax.ppermute(hidden, "dst", x_from(k)) for k in range(1, NX)]

    src = lax.axis_index("src")
    dst = lax.axis_index("dst")
    pairs = block_pairs.reshape(-1)
    scal = jnp.concatenate([pairs, jnp.stack([src, dst]).astype(jnp.int32)])

    row = block_pairs.reshape(OWNERS, SLOTS).T.astype(F32)
    row = jnp.pad(row, ((0, HEADS - SLOTS), (0, BLK - OWNERS)))[None]
    told = jnp.concatenate([own_target, row], axis=0)
    told = lax.all_to_all(jnp.broadcast_to(told[None], (OWNERS,) + told.shape), "src", 0, 0)
    every_pair = told[:, NBD, :SLOTS, :OWNERS].astype(jnp.int32).reshape(OWNERS * SLOTS, OWNERS)

    pieces = []
    for piece in along_x:
        pieces += [piece, lax.ppermute(piece, "dst", core_from(1))]
    masks = mask_bias(masks)
    token = gate(*pieces, masks)

    made, parts = [], []
    source = pieces
    for step, offsets in enumerate(PLAN):
        made.append(slots(offsets, scal, token, masks, told, att, source))
        if step == 0:
            source = made[0][NY]
        parts.append(
            [made[-1][0]] + [lax.ppermute(made[-1][k], "src", y_from(-k)) for k in range(1, NY)]
        )
    coming = {offset: () for offset in (0, *NEXT)}
    for step, offsets in enumerate(PLAN):
        work = [(offset, len(coming[offset])) for offset in offsets if offset != 0]
        if not work:
            break
        if PLAN[step + 1 : step + 2] == ((0,),):
            parts[step][0], parts[step + 1][1] = lax.optimization_barrier(
                (parts[step][0], parts[step + 1][1])
            )
        dense = sum((coming[offset] for offset, _ in work), ())
        sent = merge_group(work, scal, every_pair, parts[step], dense)
        for (offset, _), chunk in zip(work, sent, strict=True):
            hop = lax.ppermute(chunk, "src", z_from(NEXT[offset] - offset))
            coming[NEXT[offset]] += (hop,)
    home = merge_home(scal, every_pair, parts[-1], self_logit, hidden)
    return finish(coming[0], home, bias)


def solution(mesh):
    placed_at = (
        P(("dst", "src"), None),
        P(),
        P(),
        P(),
        P(),
        P("src", "dst", None, None),
        P("src", "dst", None, None, None, None),
    )
    return jax.shard_map(
        body, mesh=mesh, in_specs=placed_at, out_specs=P(("dst", "src"), None), check_vma=False
    )
```

```python
import functools

import jax
import jax.numpy as jnp
from jax import lax
from jax.experimental import pallas as pl
from jax.experimental.pallas import tpu as pltpu
from jax.sharding import PartitionSpec as P

HEADS = 4
HEAD = 64
FEAT = HEADS * HEAD
BLK = 128
NBD = 4
SLOTS = 2
NY, NZ, NX, NC = 4, 8, 4, 2
LOG_NZ = 3
PIECES = NX * NC
SRC_BLOCKS = NBD * PIECES
OWNERS = NY * NZ
PAIRS = OWNERS * SLOTS
ROWS = FEAT + 16
GATE_COST = 1400_000_000
LOG2E = 1.4426950408889634
EMPTY = -(2.0**100)
F32 = jnp.float32
BF16 = jnp.bfloat16
VMEM = pl.BlockSpec(memory_space=pltpu.VMEM)
ANY = pl.BlockSpec(memory_space=pl.ANY)


def params(**more):
    return pltpu.CompilerParams(vmem_limit_bytes=46 * 1024 * 1024, **more)


def leaky(values):
    return jnp.maximum(values, 0.2 * values)


def y_from(k):
    return [(y * NZ + z, (y - k) % NY * NZ + z) for y in range(NY) for z in range(NZ)]


def z_from(k):
    return [(y * NZ + z, y * NZ + (z - k) % NZ) for y in range(NY) for z in range(NZ)]


def x_from(k):
    return [(x * NC + c, (x - k) % NX * NC + c) for x in range(NX) for c in range(NC)]


def core_from(k):
    return [(x * NC + c, x * NC + (c - k) % NC) for x in range(NX) for c in range(NC)]


PLAN = ((4,), (3, -3), (2, -2), (1, -1, 0))
NEXT = {4: 3, 3: 2, 2: 1, 1: 0, -3: -2, -2: -1, -1: 0}


def head_sums(products):
    return jnp.concatenate(
        [jnp.sum(products[h * HEAD : (h + 1) * HEAD], axis=0, keepdims=True) for h in range(HEADS)],
        axis=0,
    )


def prepare_kernel(x_ref, both_ref, hidden_ref, target_ref, self_ref, att_ref):
    att_src = jnp.broadcast_to(both_ref[0:1] * LOG2E, (BLK, FEAT)).T
    att_dst = jnp.broadcast_to(both_ref[1:2] * LOG2E, (BLK, FEAT)).T
    att_ref[...] = att_src
    for b in range(NBD):
        wide = x_ref[b * BLK : (b + 1) * BLK, :].astype(F32).T
        hidden_ref[b] = wide.astype(BF16)
        source = head_sums(wide * att_src)
        target = head_sums(wide * att_dst)
        target_ref[b] = target
        self_ref[b] = leaky(target + source)


def prepare(hidden, att_src, att_dst):
    return pl.pallas_call(
        prepare_kernel,
        out_shape=(
            jax.ShapeDtypeStruct((NBD, FEAT, BLK), BF16),
            jax.ShapeDtypeStruct((NBD, HEADS, BLK), F32),
            jax.ShapeDtypeStruct((NBD, HEADS, BLK), F32),
            jax.ShapeDtypeStruct((FEAT, BLK), F32),
        ),
        in_specs=[VMEM] * 2,
        out_specs=(VMEM,) * 4,
        compiler_params=params(),
        name="prepare",
    )(hidden, jnp.stack([att_src, att_dst]))


def gate_kernel(*refs):
    refs[-1][...] = jnp.zeros((8, BLK), F32)


def gate(*arrays):
    return pl.pallas_call(
        gate_kernel,
        out_shape=jax.ShapeDtypeStruct((8, BLK), F32),
        in_specs=[ANY] * len(arrays),
        out_specs=VMEM,
        compiler_params=params(),
        cost_estimate=pl.CostEstimate(flops=GATE_COST, bytes_accessed=1000, transcendentals=0),
        name="gate",
    )(*arrays)


def mask_kernel(mask_ref, out_ref):
    for n in range(mask_ref.shape[0]):
        for t in range(SLOTS):
            bias = jnp.where(mask_ref[n, t] > 0, 0.0, EMPTY).astype(F32)
            out_ref[n, t] = bias.T.astype(BF16)


def mask_bias(masks):
    step = 4
    spec = pl.BlockSpec((step, SLOTS, BLK, BLK), lambda i: (i, 0, 0, 0))
    return pl.pallas_call(
        mask_kernel,
        grid=(OWNERS // step,),
        out_shape=jax.ShapeDtypeStruct((OWNERS, SLOTS, BLK, BLK), BF16),
        in_specs=[spec],
        out_specs=spec,
        compiler_params=params(),
        cost_estimate=pl.CostEstimate(
            flops=PAIRS * BLK * BLK * 8, bytes_accessed=PAIRS * BLK * BLK * 6, transcendentals=0
        ),
        name="mask_bias",
    )(masks)


def owner_of(scal, k, offset):
    src = scal[PAIRS]
    return ((((src >> LOG_NZ) + k) & (NY - 1)) << LOG_NZ) | ((src + offset) & (NZ - 1))


def halves(values):
    high = values.astype(BF16).astype(F32)
    return high, (values - high).astype(BF16).astype(F32)


def slot_partial(hidden, att, bias, target, out_ref, place):
    sources = head_sums(hidden.astype(F32) * att)
    sources = jnp.concatenate([sources, sources], axis=0).T
    bounds, totals = [], []
    for h in range(HEADS):
        masked = sources[:, h : h + 1] + bias
        top = jnp.max(masked, axis=0, keepdims=True)
        own = target[h : h + 1]
        high, low = halves(leaky(own + top))
        bound = high + low
        weights = jnp.exp2(
            jnp.maximum(masked + (own - bound), 0.2 * masked + (0.2 * own - bound))
        )
        bounds.append((high, low))
        totals.append(halves(jnp.sum(weights, axis=0, keepdims=True)))
        out_ref[place + (pl.ds(h * HEAD, HEAD), slice(None))] = jnp.dot(
            hidden[h * HEAD : (h + 1) * HEAD], weights.astype(BF16), preferred_element_type=F32
        ).astype(BF16)
    rows = [b[0] for b in bounds] + [t[0] for t in totals]
    rows += [b[1] for b in bounds] + [t[1] for t in totals]
    out_ref[place + (pl.ds(FEAT, 16), slice(None))] = jnp.concatenate(rows, axis=0).astype(BF16)


def slots_kernel(offsets, first, scal, token, targets, att, bias, *rest):
    del token
    if first:
        sources, (*outs, hidden, made, sems) = rest[:PIECES], rest[PIECES:]
        copies = [
            pltpu.make_async_copy(sources[n], hidden.at[pl.ds(n * NBD, NBD)], sems.at[n])
            for n in range(PIECES)
        ]
        for copy in copies:
            copy.start()
        for copy in copies:
            copy.wait()
    else:
        hidden, *outs, made = rest
    dst = scal[PAIRS + 1]
    together = made.shape[0]

    def some(step, carry):
        for part in range(together):
            for n, offset in enumerate(offsets):
                owner = owner_of(scal, step * together + part, offset)
                for t in range(SLOTS):
                    pair = scal[owner * SLOTS + t]
                    block = pair & (SRC_BLOCKS - 1)
                    place = pair >> (SRC_BLOCKS.bit_length() - 1)
                    holder = block >> (NBD.bit_length() - 1)
                    dx = ((holder >> 1) - (dst >> 1)) & (NX - 1)
                    dc = (holder ^ dst) & (NC - 1)
                    held = ((dx * NC + dc) * NBD) | (block & (NBD - 1))
                    slot_partial(
                        hidden[held], att[...], bias[owner, t].astype(F32), targets[owner, place], made, (part, n, t)
                    )
        for other in range(NY // together):

            @pl.when(step == other)
            def _(other=other):
                for part in range(together):
                    outs[other * together + part][...] = made[part]

        return carry

    lax.fori_loop(0, NY // together, some, 0)


def slots(offsets, scal, token, bias, targets, att, source):
    first = isinstance(source, list)
    shape = (len(offsets), SLOTS, ROWS, BLK)
    out_shape = (jax.ShapeDtypeStruct(shape, BF16),) * NY
    scratch = [pltpu.VMEM((max(1, 4 // len(offsets)),) + shape, BF16)]
    if first:
        out_shape += (jax.ShapeDtypeStruct((SRC_BLOCKS, FEAT, BLK), BF16),)
        scratch.append(pltpu.SemaphoreType.DMA((PIECES,)))
    return pl.pallas_call(
        functools.partial(slots_kernel, offsets, first),
        out_shape=out_shape,
        in_specs=[SMEM, ANY, VMEM, VMEM, VMEM] + ([ANY] * PIECES if first else [VMEM]),
        out_specs=(VMEM,) * len(out_shape),
        scratch_shapes=scratch,
        compiler_params=params(),
        cost_estimate=pl.CostEstimate(flops=1000, bytes_accessed=1000, transcendentals=0),
        name="slots",
    )(scal, token, targets, att, bias, *(source if first else [source]))


def bound_total(ref, place):
    rows = ref[place + (pl.ds(FEAT, 16), slice(None))].astype(F32)
    both = rows[:8] + rows[8:]
    return both[:HEADS], both[HEADS:]


def merge(slot_list, dense, bounds, totals, sums, given=None):
    for b in range(NBD):
        top = jnp.full((HEADS, BLK), EMPTY, F32) if given is None else given[0][b]
        for ref in dense:
            top = jnp.maximum(top, bound_total(ref, (b,))[0])
        bounds[b] = top
    for ref, index, place in slot_list:
        bounds[place] = jnp.maximum(bounds[place], bound_total(ref, index)[0])
    for b in range(NBD):
        total = jnp.zeros((HEADS, BLK), F32)
        terms = []
        if given is not None:
            factor = jnp.exp2(given[0][b] - bounds[b])
            total += factor if given[1] is None else given[1][b] * factor
            terms.append((given[2], (b,), factor))
        for ref in dense:
            bound, more = bound_total(ref, (b,))
            factor = jnp.exp2(bound - bounds[b])
            total += more * factor
            terms.append((ref, (b,), factor))
        totals[b] = total
        for h in range(HEADS):
            rows = pl.ds(h * HEAD, HEAD)
            value = jnp.zeros((HEAD, BLK), F32)
            for ref, index, factor in terms:
                value += ref[index + (rows, slice(None))].astype(F32) * factor[h : h + 1]
            sums[b, rows, :] = value
    for ref, index, place in slot_list:
        bound, more = bound_total(ref, index)
        factor = jnp.exp2(bound - bounds[place])
        totals[place] += more * factor
        for h in range(HEADS):
            rows = pl.ds(h * HEAD, HEAD)
            sums[place, rows, :] += (
                ref[index + (rows, slice(None))].astype(F32) * factor[h : h + 1]
            )


def placed(scal, every_pair, offset, refs, n):
    owner = owner_of(scal, 0, offset)
    found = []
    for k in range(NY):
        maker = owner_of(scal, -k, 0)
        for t in range(SLOTS):
            place = every_pair[maker * SLOTS + t, owner] >> (SRC_BLOCKS.bit_length() - 1)
            found.append((refs[k], (n, t), place))
    return found


def write_dense(out, bounds, totals, sums):
    for b in range(NBD):
        out[b, pl.ds(0, FEAT), :] = sums[b].astype(BF16)
        both = halves(jnp.concatenate([bounds[b], totals[b]], axis=0))
        out[b, pl.ds(FEAT, 16), :] = jnp.concatenate(both, axis=0).astype(BF16)


def merge_kernel(work, scal, every_pair, *refs):
    parts, refs = refs[:NY], refs[NY:]
    n_dense = sum(w[1] for w in work)
    dense, refs = refs[:n_dense], refs[n_dense:]
    outs, (bounds, totals, sums) = refs[: len(work)], refs[len(work) :]
    for n, (out, (offset, count)) in enumerate(zip(outs, work, strict=True)):
        mine, dense = dense[:count], dense[count:]
        merge(placed(scal, every_pair, offset, parts, n), mine, bounds, totals, sums)
        write_dense(out, bounds, totals, sums)


SUMS = ((NBD, HEADS, BLK), (NBD, HEADS, BLK), (NBD, FEAT, BLK))
SMEM = pl.BlockSpec(memory_space=pltpu.SMEM)


def merge_group(work, scal, every_pair, parts, dense):
    return pl.pallas_call(
        functools.partial(merge_kernel, work),
        out_shape=(jax.ShapeDtypeStruct((NBD, ROWS, BLK), BF16),) * len(work),
        in_specs=[SMEM] * 2 + [VMEM] * (NY + len(dense)),
        out_specs=(VMEM,) * len(work),
        scratch_shapes=[pltpu.VMEM(shape, F32) for shape in SUMS],
        compiler_params=params(),
        cost_estimate=pl.CostEstimate(flops=1000, bytes_accessed=1000, transcendentals=0),
        name="merge",
    )(scal, every_pair, *parts, *dense)


def home_kernel(n, scal, every_pair, *refs):
    parts, (self_ref, hidden_ref, bounds, totals, sums) = refs[:NY], refs[NY:]
    found = placed(scal, every_pair, 0, parts, n)
    merge(found, (), bounds, totals, sums, (self_ref, None, hidden_ref))


def merge_home(scal, every_pair, parts, self_logit, hidden):
    return pl.pallas_call(
        functools.partial(home_kernel, PLAN[-1].index(0)),
        out_shape=tuple(jax.ShapeDtypeStruct(shape, F32) for shape in SUMS),
        in_specs=[SMEM] * 2 + [VMEM] * (NY + 2),
        out_specs=(VMEM,) * 3,
        compiler_params=params(),
        cost_estimate=pl.CostEstimate(flops=1000, bytes_accessed=1000, transcendentals=0),
        name="merge_home",
    )(scal, every_pair, *parts, self_logit, hidden)


def finish_kernel(*refs):
    dense, refs = refs[:-8], refs[-8:]
    home_bounds, home_totals, home_sums, bias_ref, out, bounds, totals, sums = refs
    merge((), dense, bounds, totals, sums, (home_bounds, home_totals, home_sums))
    for b in range(NBD):
        scale = 1.0 / totals[b]
        value = jnp.concatenate(
            [sums[b, pl.ds(h * HEAD, HEAD), :] * scale[h : h + 1] for h in range(HEADS)], axis=0
        )
        value = value.T + bias_ref[...]
        out[pl.ds(b * BLK, BLK), :] = jnp.where(
            value > 0, value, jnp.exp(jnp.minimum(value, 0.0)) - 1.0
        )


def finish(dense, home, bias):
    return pl.pallas_call(
        finish_kernel,
        out_shape=jax.ShapeDtypeStruct((NBD * BLK, FEAT), F32),
        in_specs=[VMEM] * (len(dense) + 4),
        out_specs=VMEM,
        scratch_shapes=[pltpu.VMEM(shape, F32) for shape in SUMS],
        compiler_params=params(),
        name="finish",
    )(*dense, *home, bias.reshape(1, FEAT))


def slots_list(*args):
    return list(slots(*args))


def body(features, weight, att_src, att_dst, bias, block_pairs, edge_masks):
    masks = edge_masks.reshape(OWNERS, SLOTS, BLK, BLK)
    hidden = jnp.dot(features, weight, preferred_element_type=F32).astype(BF16)
    hidden, own_target, self_logit, att = prepare(hidden, att_src, att_dst)
    along_x = [hidden] + [lax.ppermute(hidden, "dst", x_from(k)) for k in range(1, NX)]

    src = lax.axis_index("src")
    dst = lax.axis_index("dst")
    pairs = block_pairs.reshape(-1)
    scal = jnp.concatenate([pairs, jnp.stack([src, dst]).astype(jnp.int32)])

    row = block_pairs.reshape(OWNERS, SLOTS).T.astype(F32)
    row = jnp.pad(row, ((0, HEADS - SLOTS), (0, BLK - OWNERS)))[None]
    told = jnp.concatenate([own_target, row], axis=0)
    told = lax.all_to_all(jnp.broadcast_to(told[None], (OWNERS,) + told.shape), "src", 0, 0)
    every_pair = told[:, NBD, :SLOTS, :OWNERS].astype(jnp.int32).reshape(OWNERS * SLOTS, OWNERS)

    pieces = []
    for piece in along_x:
        pieces += [piece, lax.ppermute(piece, "dst", core_from(1))]
    masks = mask_bias(masks)
    token = gate(*pieces, masks)

    made, parts = [], []
    source = pieces
    for step, offsets in enumerate(PLAN):
        made.append(slots_list(offsets, scal, token, masks, told, att, source))
        if step == 0:
            source = made[0][NY]
        parts.append(
            [made[-1][0]] + [lax.ppermute(made[-1][k], "src", y_from(-k)) for k in range(1, NY)]
        )
    coming = {offset: () for offset in (0, *NEXT)}
    for step, offsets in enumerate(PLAN):
        work = [(offset, len(coming[offset])) for offset in offsets if offset != 0]
        if not work:
            break
        if PLAN[step + 1 : step + 2] == ((0,),):
            parts[step][0], parts[step + 1][1] = lax.optimization_barrier(
                (parts[step][0], parts[step + 1][1])
            )
        if step == 1:
            parts[1][0], made[3][0] = lax.optimization_barrier((parts[1][0], made[3][0]))
        dense = sum((coming[offset] for offset, _ in work), ())
        sent = merge_group(work, scal, every_pair, parts[step], dense)
        for (offset, _), chunk in zip(work, sent, strict=True):
            hop = lax.ppermute(chunk, "src", z_from(NEXT[offset] - offset))
            coming[NEXT[offset]] += (hop,)
    home = merge_home(scal, every_pair, parts[-1], self_logit, hidden)
    return finish(coming[0], home, bias)


def solution(mesh):
    placed_at = (
        P(("dst", "src"), None),
        P(),
        P(),
        P(),
        P(),
        P("src", "dst", None, None),
        P("src", "dst", None, None, None, None),
    )
    return jax.shard_map(
        body, mesh=mesh, in_specs=placed_at, out_specs=P(("dst", "src"), None), check_vma=False
    )
```

```python
import functools

import jax
import jax.numpy as jnp
from jax import lax
from jax.experimental import pallas as pl
from jax.experimental.pallas import tpu as pltpu
from jax.sharding import PartitionSpec as P

HEADS = 4
HEAD = 64
FEAT = HEADS * HEAD
BLK = 128
NBD = 4
SLOTS = 2
NY, NZ, NX, NC = 4, 8, 4, 2
LOG_NZ = 3
PIECES = NX * NC
SRC_BLOCKS = NBD * PIECES
OWNERS = NY * NZ
PAIRS = OWNERS * SLOTS
ROWS = FEAT + 16
GATE_COST = 1400_000_000
LOG2E = 1.4426950408889634
EMPTY = -(2.0**100)
F32 = jnp.float32
BF16 = jnp.bfloat16
VMEM = pl.BlockSpec(memory_space=pltpu.VMEM)
ANY = pl.BlockSpec(memory_space=pl.ANY)


def params(**more):
    return pltpu.CompilerParams(vmem_limit_bytes=46 * 1024 * 1024, **more)


def leaky(values):
    return jnp.maximum(values, 0.2 * values)


def y_from(k):
    return [(y * NZ + z, (y - k) % NY * NZ + z) for y in range(NY) for z in range(NZ)]


def z_from(k):
    return [(y * NZ + z, y * NZ + (z - k) % NZ) for y in range(NY) for z in range(NZ)]


def x_from(k):
    return [(x * NC + c, (x - k) % NX * NC + c) for x in range(NX) for c in range(NC)]


def core_from(k):
    return [(x * NC + c, x * NC + (c - k) % NC) for x in range(NX) for c in range(NC)]


PLAN = ((4,), (3, -3), (2, -2), (1, -1, 0))
NEXT = {4: 3, 3: 2, 2: 1, 1: 0, -3: -2, -2: -1, -1: 0}


def head_sums(products):
    return jnp.concatenate(
        [jnp.sum(products[h * HEAD : (h + 1) * HEAD], axis=0, keepdims=True) for h in range(HEADS)],
        axis=0,
    )


def prepare_kernel(x_ref, both_ref, hidden_ref, target_ref, self_ref, att_ref):
    att_src = jnp.broadcast_to(both_ref[0:1] * LOG2E, (BLK, FEAT)).T
    att_dst = jnp.broadcast_to(both_ref[1:2] * LOG2E, (BLK, FEAT)).T
    att_ref[...] = att_src
    for b in range(NBD):
        wide = x_ref[b * BLK : (b + 1) * BLK, :].astype(F32).T
        hidden_ref[b] = wide.astype(BF16)
        source = head_sums(wide * att_src)
        target = head_sums(wide * att_dst)
        target_ref[b] = target
        self_ref[b] = leaky(target + source)


def prepare(hidden, att_src, att_dst):
    return pl.pallas_call(
        prepare_kernel,
        out_shape=(
            jax.ShapeDtypeStruct((NBD, FEAT, BLK), BF16),
            jax.ShapeDtypeStruct((NBD, HEADS, BLK), F32),
            jax.ShapeDtypeStruct((NBD, HEADS, BLK), F32),
            jax.ShapeDtypeStruct((FEAT, BLK), F32),
        ),
        in_specs=[VMEM] * 2,
        out_specs=(VMEM,) * 4,
        compiler_params=params(),
        name="prepare",
    )(hidden, jnp.stack([att_src, att_dst]))


def gate_kernel(*refs):
    refs[-1][...] = jnp.zeros((8, BLK), F32)


def gate(*arrays):
    return pl.pallas_call(
        gate_kernel,
        out_shape=jax.ShapeDtypeStruct((8, BLK), F32),
        in_specs=[ANY] * len(arrays),
        out_specs=VMEM,
        compiler_params=params(),
        cost_estimate=pl.CostEstimate(flops=GATE_COST, bytes_accessed=1000, transcendentals=0),
        name="gate",
    )(*arrays)


def mask_kernel(mask_ref, out_ref):
    for n in range(mask_ref.shape[0]):
        for t in range(SLOTS):
            bias = jnp.where(mask_ref[n, t] > 0, 0.0, EMPTY).astype(F32)
            out_ref[n, t] = bias.T.astype(BF16)


def mask_bias(masks):
    step = 4
    spec = pl.BlockSpec((step, SLOTS, BLK, BLK), lambda i: (i, 0, 0, 0))
    return pl.pallas_call(
        mask_kernel,
        grid=(OWNERS // step,),
        out_shape=jax.ShapeDtypeStruct((OWNERS, SLOTS, BLK, BLK), BF16),
        in_specs=[spec],
        out_specs=spec,
        compiler_params=params(),
        cost_estimate=pl.CostEstimate(
            flops=PAIRS * BLK * BLK * 8, bytes_accessed=PAIRS * BLK * BLK * 6, transcendentals=0
        ),
        name="mask_bias",
    )(masks)


def owner_of(scal, k, offset):
    src = scal[PAIRS]
    return ((((src >> LOG_NZ) + k) & (NY - 1)) << LOG_NZ) | ((src + offset) & (NZ - 1))


def halves(values):
    high = values.astype(BF16).astype(F32)
    return high, (values - high).astype(BF16).astype(F32)


def slot_partial(hidden, att, bias, target, out_ref, place):
    sources = head_sums(hidden.astype(F32) * att)
    sources = jnp.concatenate([sources, sources], axis=0).T
    bounds, totals = [], []
    for h in range(HEADS):
        masked = sources[:, h : h + 1] + bias
        top = jnp.max(masked, axis=0, keepdims=True)
        own = target[h : h + 1]
        high, low = halves(leaky(own + top))
        bound = high + low
        weights = jnp.exp2(
            jnp.maximum(masked + (own - bound), 0.2 * masked + (0.2 * own - bound))
        )
        bounds.append((high, low))
        totals.append(halves(jnp.sum(weights, axis=0, keepdims=True)))
        out_ref[place + (pl.ds(h * HEAD, HEAD), slice(None))] = jnp.dot(
            hidden[h * HEAD : (h + 1) * HEAD], weights.astype(BF16), preferred_element_type=F32
        ).astype(BF16)
    rows = [b[0] for b in bounds] + [t[0] for t in totals]
    rows += [b[1] for b in bounds] + [t[1] for t in totals]
    out_ref[place + (pl.ds(FEAT, 16), slice(None))] = jnp.concatenate(rows, axis=0).astype(BF16)


def slots_kernel(offsets, first, scal, token, targets, att, bias, *rest):
    del token
    if first:
        sources, (*outs, hidden, made, sems) = rest[:PIECES], rest[PIECES:]
        copies = [
            pltpu.make_async_copy(sources[n], hidden.at[pl.ds(n * NBD, NBD)], sems.at[n])
            for n in range(PIECES)
        ]
        for copy in copies:
            copy.start()
        for copy in copies:
            copy.wait()
    else:
        hidden, *outs, made = rest
    dst = scal[PAIRS + 1]
    together = made.shape[0]

    def some(step, carry):
        for part in range(together):
            for n, offset in enumerate(offsets):
                owner = owner_of(scal, step * together + part, offset)
                for t in range(SLOTS):
                    pair = scal[owner * SLOTS + t]
                    block = pair & (SRC_BLOCKS - 1)
                    place = pair >> (SRC_BLOCKS.bit_length() - 1)
                    holder = block >> (NBD.bit_length() - 1)
                    dx = ((holder >> 1) - (dst >> 1)) & (NX - 1)
                    dc = (holder ^ dst) & (NC - 1)
                    held = ((dx * NC + dc) * NBD) | (block & (NBD - 1))
                    slot_partial(
                        hidden[held], att[...], bias[owner, t].astype(F32), targets[owner, place], made, (part, n, t)
                    )
        for other in range(NY // together):

            @pl.when(step == other)
            def _(other=other):
                for part in range(together):
                    outs[other * together + part][...] = made[part]

        return carry

    lax.fori_loop(0, NY // together, some, 0)


def slots(offsets, scal, token, bias, targets, att, source):
    first = isinstance(source, list)
    shape = (len(offsets), SLOTS, ROWS, BLK)
    out_shape = (jax.ShapeDtypeStruct(shape, BF16),) * NY
    scratch = [pltpu.VMEM((max(1, 4 // len(offsets)),) + shape, BF16)]
    if first:
        out_shape += (jax.ShapeDtypeStruct((SRC_BLOCKS, FEAT, BLK), BF16),)
        scratch.append(pltpu.SemaphoreType.DMA((PIECES,)))
    return pl.pallas_call(
        functools.partial(slots_kernel, offsets, first),
        out_shape=out_shape,
        in_specs=[SMEM, ANY, VMEM, VMEM, VMEM] + ([ANY] * PIECES if first else [VMEM]),
        out_specs=(VMEM,) * len(out_shape),
        scratch_shapes=scratch,
        compiler_params=params(),
        cost_estimate=pl.CostEstimate(flops=1000, bytes_accessed=1000, transcendentals=0),
        name="slots",
    )(scal, token, targets, att, bias, *(source if first else [source]))


def bound_total(ref, place):
    rows = ref[place + (pl.ds(FEAT, 16), slice(None))].astype(F32)
    both = rows[:8] + rows[8:]
    return both[:HEADS], both[HEADS:]


def merge(slot_list, dense, bounds, totals, sums, given=None):
    for b in range(NBD):
        top = jnp.full((HEADS, BLK), EMPTY, F32) if given is None else given[0][b]
        for ref in dense:
            top = jnp.maximum(top, bound_total(ref, (b,))[0])
        bounds[b] = top
    for ref, index, place in slot_list:
        bounds[place] = jnp.maximum(bounds[place], bound_total(ref, index)[0])
    for b in range(NBD):
        total = jnp.zeros((HEADS, BLK), F32)
        terms = []
        if given is not None:
            factor = jnp.exp2(given[0][b] - bounds[b])
            total += factor if given[1] is None else given[1][b] * factor
            terms.append((given[2], (b,), factor))
        for ref in dense:
            bound, more = bound_total(ref, (b,))
            factor = jnp.exp2(bound - bounds[b])
            total += more * factor
            terms.append((ref, (b,), factor))
        totals[b] = total
        for h in range(HEADS):
            rows = pl.ds(h * HEAD, HEAD)
            value = jnp.zeros((HEAD, BLK), F32)
            for ref, index, factor in terms:
                value += ref[index + (rows, slice(None))].astype(F32) * factor[h : h + 1]
            sums[b, rows, :] = value
    for ref, index, place in slot_list:
        bound, more = bound_total(ref, index)
        factor = jnp.exp2(bound - bounds[place])
        totals[place] += more * factor
        for h in range(HEADS):
            rows = pl.ds(h * HEAD, HEAD)
            sums[place, rows, :] += (
                ref[index + (rows, slice(None))].astype(F32) * factor[h : h + 1]
            )


def placed(scal, every_pair, offset, refs, n):
    owner = owner_of(scal, 0, offset)
    found = []
    for k in range(NY):
        maker = owner_of(scal, -k, 0)
        for t in range(SLOTS):
            place = every_pair[(maker >> LOG_NZ) * SLOTS + t, owner] >> (SRC_BLOCKS.bit_length() - 1)
            found.append((refs[k], (n, t), place))
    return found


def write_dense(out, bounds, totals, sums):
    for b in range(NBD):
        out[b, pl.ds(0, FEAT), :] = sums[b].astype(BF16)
        both = halves(jnp.concatenate([bounds[b], totals[b]], axis=0))
        out[b, pl.ds(FEAT, 16), :] = jnp.concatenate(both, axis=0).astype(BF16)


def merge_kernel(work, scal, every_pair, *refs):
    parts, refs = refs[:NY], refs[NY:]
    n_dense = sum(w[1] for w in work)
    dense, refs = refs[:n_dense], refs[n_dense:]
    outs, (bounds, totals, sums) = refs[: len(work)], refs[len(work) :]
    for n, (out, (offset, count)) in enumerate(zip(outs, work, strict=True)):
        mine, dense = dense[:count], dense[count:]
        merge(placed(scal, every_pair, offset, parts, n), mine, bounds, totals, sums)
        write_dense(out, bounds, totals, sums)


SUMS = ((NBD, HEADS, BLK), (NBD, HEADS, BLK), (NBD, FEAT, BLK))
SMEM = pl.BlockSpec(memory_space=pltpu.SMEM)


def merge_group(work, scal, every_pair, parts, dense):
    return pl.pallas_call(
        functools.partial(merge_kernel, work),
        out_shape=(jax.ShapeDtypeStruct((NBD, ROWS, BLK), BF16),) * len(work),
        in_specs=[SMEM] * 2 + [VMEM] * (NY + len(dense)),
        out_specs=(VMEM,) * len(work),
        scratch_shapes=[pltpu.VMEM(shape, F32) for shape in SUMS],
        compiler_params=params(),
        cost_estimate=pl.CostEstimate(flops=1000, bytes_accessed=1000, transcendentals=0),
        name="merge",
    )(scal, every_pair, *parts, *dense)


def home_kernel(n, scal, every_pair, *refs):
    parts, (self_ref, hidden_ref, bounds, totals, sums) = refs[:NY], refs[NY:]
    found = placed(scal, every_pair, 0, parts, n)
    merge(found, (), bounds, totals, sums, (self_ref, None, hidden_ref))


def merge_home(scal, every_pair, parts, self_logit, hidden):
    return pl.pallas_call(
        functools.partial(home_kernel, PLAN[-1].index(0)),
        out_shape=tuple(jax.ShapeDtypeStruct(shape, F32) for shape in SUMS),
        in_specs=[SMEM] * 2 + [VMEM] * (NY + 2),
        out_specs=(VMEM,) * 3,
        compiler_params=params(),
        cost_estimate=pl.CostEstimate(flops=1000, bytes_accessed=1000, transcendentals=0),
        name="merge_home",
    )(scal, every_pair, *parts, self_logit, hidden)


def finish_kernel(*refs):
    dense, refs = refs[:-8], refs[-8:]
    home_bounds, home_totals, home_sums, bias_ref, out, bounds, totals, sums = refs
    merge((), dense, bounds, totals, sums, (home_bounds, home_totals, home_sums))
    for b in range(NBD):
        scale = 1.0 / totals[b]
        value = jnp.concatenate(
            [sums[b, pl.ds(h * HEAD, HEAD), :] * scale[h : h + 1] for h in range(HEADS)], axis=0
        )
        value = value.T + bias_ref[...]
        out[pl.ds(b * BLK, BLK), :] = jnp.where(
            value > 0, value, jnp.exp(jnp.minimum(value, 0.0)) - 1.0
        )


def finish(dense, home, bias):
    return pl.pallas_call(
        finish_kernel,
        out_shape=jax.ShapeDtypeStruct((NBD * BLK, FEAT), F32),
        in_specs=[VMEM] * (len(dense) + 4),
        out_specs=VMEM,
        scratch_shapes=[pltpu.VMEM(shape, F32) for shape in SUMS],
        compiler_params=params(),
        name="finish",
    )(*dense, *home, bias.reshape(1, FEAT))


def slots_list(*args):
    return list(slots(*args))


def body(features, weight, att_src, att_dst, bias, block_pairs, edge_masks):
    masks = edge_masks.reshape(OWNERS, SLOTS, BLK, BLK)
    hidden = jnp.dot(features, weight, preferred_element_type=F32).astype(BF16)
    hidden, own_target, self_logit, att = prepare(hidden, att_src, att_dst)
    along_x = [hidden] + [lax.ppermute(hidden, "dst", x_from(k)) for k in range(1, NX)]

    src = lax.axis_index("src")
    dst = lax.axis_index("dst")
    pairs = block_pairs.reshape(-1)
    scal = jnp.concatenate([pairs, jnp.stack([src, dst]).astype(jnp.int32)])

    row = block_pairs.reshape(OWNERS, SLOTS).T.astype(F32)
    row = jnp.pad(row, ((0, HEADS - SLOTS), (0, BLK - OWNERS)))[None]
    told = jnp.concatenate([own_target, row], axis=0)
    told = lax.all_to_all(jnp.broadcast_to(told[None], (OWNERS,) + told.shape), "src", 0, 0)
    every_pair = told[:, NBD, :SLOTS, :OWNERS].astype(jnp.int32).reshape(OWNERS * SLOTS, OWNERS)
    every_pair = lax.optimization_barrier(every_pair).reshape(NY, NZ, SLOTS, OWNERS)
    every_pair = lax.dynamic_index_in_dim(every_pair, src % NZ, 1, keepdims=False)
    every_pair = every_pair.reshape(NY * SLOTS, OWNERS)

    pieces = []
    for piece in along_x:
        pieces += [piece, lax.ppermute(piece, "dst", core_from(1))]
    masks = mask_bias(masks)
    token = gate(*pieces, masks)

    coming = {offset: () for offset in (0, *NEXT)}

    def travel(made):
        return [made[0]] + [lax.ppermute(made[k], "src", y_from(-k)) for k in range(1, NY)]

    def sums(step):
        work = [(offset, len(coming[offset])) for offset in PLAN[step] if offset != 0]
        dense = sum((coming[offset] for offset, _ in work), ())
        return work, list(merge_group(work, scal, every_pair, parts[step], dense))

    def send(work, chunks):
        for (offset, _), chunk in zip(work, chunks, strict=True):
            hop = lax.ppermute(chunk, "src", z_from(NEXT[offset] - offset))
            coming[NEXT[offset]] += (hop,)

    parts = [None] * len(PLAN)
    first = slots(PLAN[0], scal, token, masks, told, att, pieces)
    laid = first[NY]
    parts[0] = travel(first[:NY])
    parts[1] = travel(slots(PLAN[1], scal, token, masks, told, att, laid))
    later, parts[0][1] = lax.optimization_barrier((token, parts[0][1]))
    third = list(slots(PLAN[2], scal, later, masks, told, att, laid))
    parts[0][0], third[0] = lax.optimization_barrier((parts[0][0], third[0]))
    work, chunks = sums(0)
    later, chunks[0] = lax.optimization_barrier((token, chunks[0]))
    send(work, chunks)
    last = list(slots(PLAN[3], scal, later, masks, told, att, laid))
    parts[2] = travel(third)
    parts[3] = travel(last)
    parts[1][0], last[0] = lax.optimization_barrier((parts[1][0], last[0]))
    for step in range(1, len(PLAN)):
        send(*sums(step))
    home = merge_home(scal, every_pair, parts[-1], self_logit, hidden)
    return finish(coming[0], home, bias)


def solution(mesh):
    placed_at = (
        P(("dst", "src"), None),
        P(),
        P(),
        P(),
        P(),
        P("src", "dst", None, None),
        P("src", "dst", None, None, None, None),
    )
    return jax.shard_map(
        body, mesh=mesh, in_specs=placed_at, out_specs=P(("dst", "src"), None), check_vma=False
    )
```

```python
import functools

import jax
import jax.numpy as jnp
from jax import lax
from jax.experimental import pallas as pl
from jax.experimental.pallas import tpu as pltpu
from jax.sharding import PartitionSpec as P

HEADS = 4
HEAD = 64
FEAT = HEADS * HEAD
BLK = 128
NBD = 4
SLOTS = 2
NY, NZ, NX, NC = 4, 8, 4, 2
LOG_NZ = 3
PIECES = NX * NC
SRC_BLOCKS = NBD * PIECES
OWNERS = NY * NZ
PAIRS = OWNERS * SLOTS
ROWS = FEAT + 16
GATE_COST = 1400_000_000
LOG2E = 1.4426950408889634
EMPTY = -(2.0**100)
F32 = jnp.float32
BF16 = jnp.bfloat16
VMEM = pl.BlockSpec(memory_space=pltpu.VMEM)
ANY = pl.BlockSpec(memory_space=pl.ANY)


def params(**more):
    return pltpu.CompilerParams(vmem_limit_bytes=46 * 1024 * 1024, **more)


def leaky(values):
    return jnp.maximum(values, 0.2 * values)


def y_from(k):
    return [(y * NZ + z, (y - k) % NY * NZ + z) for y in range(NY) for z in range(NZ)]


def z_from(k):
    return [(y * NZ + z, y * NZ + (z - k) % NZ) for y in range(NY) for z in range(NZ)]


def x_from(k):
    return [(x * NC + c, (x - k) % NX * NC + c) for x in range(NX) for c in range(NC)]


def core_from(k):
    return [(x * NC + c, x * NC + (c - k) % NC) for x in range(NX) for c in range(NC)]


PLAN = ((4,), (3, -3), (2, -2), (1, -1, 0))
NEXT = {4: 3, 3: 2, 2: 1, 1: 0, -3: -2, -2: -1, -1: 0}


def head_sums(products):
    return jnp.concatenate(
        [jnp.sum(products[h * HEAD : (h + 1) * HEAD], axis=0, keepdims=True) for h in range(HEADS)],
        axis=0,
    )


def prepare_kernel(x_ref, both_ref, hidden_ref, target_ref, self_ref, att_ref):
    att_src = jnp.broadcast_to(both_ref[0:1] * LOG2E, (BLK, FEAT)).T
    att_dst = jnp.broadcast_to(both_ref[1:2] * LOG2E, (BLK, FEAT)).T
    att_ref[...] = att_src
    for b in range(NBD):
        wide = x_ref[b * BLK : (b + 1) * BLK, :].astype(F32).T
        hidden_ref[b] = wide.astype(BF16)
        source = head_sums(wide * att_src)
        target = head_sums(wide * att_dst)
        target_ref[b] = target
        self_ref[b] = leaky(target + source)


def prepare(hidden, att_src, att_dst):
    return pl.pallas_call(
        prepare_kernel,
        out_shape=(
            jax.ShapeDtypeStruct((NBD, FEAT, BLK), BF16),
            jax.ShapeDtypeStruct((NBD, HEADS, BLK), F32),
            jax.ShapeDtypeStruct((NBD, HEADS, BLK), F32),
            jax.ShapeDtypeStruct((FEAT, BLK), F32),
        ),
        in_specs=[VMEM] * 2,
        out_specs=(VMEM,) * 4,
        compiler_params=params(),
        name="prepare",
    )(hidden, jnp.stack([att_src, att_dst]))


def gate_kernel(*refs):
    refs[-1][...] = jnp.zeros((8, BLK), F32)


def gate(*arrays):
    return pl.pallas_call(
        gate_kernel,
        out_shape=jax.ShapeDtypeStruct((8, BLK), F32),
        in_specs=[ANY] * len(arrays),
        out_specs=VMEM,
        compiler_params=params(),
        cost_estimate=pl.CostEstimate(flops=GATE_COST, bytes_accessed=1000, transcendentals=0),
        name="gate",
    )(*arrays)


def mask_kernel(mask_ref, out_ref):
    for n in range(mask_ref.shape[0]):
        for t in range(SLOTS):
            bias = jnp.where(mask_ref[n, t] > 0, 0.0, EMPTY).astype(F32)
            out_ref[n, t] = bias.T.astype(BF16)


def mask_bias(masks):
    step = 4
    spec = pl.BlockSpec((step, SLOTS, BLK, BLK), lambda i: (i, 0, 0, 0))
    return pl.pallas_call(
        mask_kernel,
        grid=(OWNERS // step,),
        out_shape=jax.ShapeDtypeStruct((OWNERS, SLOTS, BLK, BLK), BF16),
        in_specs=[spec],
        out_specs=spec,
        compiler_params=params(),
        cost_estimate=pl.CostEstimate(
            flops=PAIRS * BLK * BLK * 8, bytes_accessed=PAIRS * BLK * BLK * 6, transcendentals=0
        ),
        name="mask_bias",
    )(masks)


def owner_of(scal, k, offset):
    src = scal[PAIRS]
    return ((((src >> LOG_NZ) + k) & (NY - 1)) << LOG_NZ) | ((src + offset) & (NZ - 1))


def halves(values):
    high = values.astype(BF16).astype(F32)
    return high, (values - high).astype(BF16).astype(F32)


def slot_partial(hidden, att, bias, target, out_ref, place):
    sources = head_sums(hidden.astype(F32) * att)
    sources = jnp.concatenate([sources, sources], axis=0).T
    bounds, totals = [], []
    for h in range(HEADS):
        masked = sources[:, h : h + 1] + bias
        top = jnp.max(masked, axis=0, keepdims=True)
        own = target[h : h + 1]
        high, low = halves(leaky(own + top))
        bound = high + low
        weights = jnp.exp2(
            jnp.maximum(masked + (own - bound), 0.2 * masked + (0.2 * own - bound))
        )
        bounds.append((high, low))
        totals.append(halves(jnp.sum(weights, axis=0, keepdims=True)))
        out_ref[place + (pl.ds(h * HEAD, HEAD), slice(None))] = jnp.dot(
            hidden[h * HEAD : (h + 1) * HEAD], weights.astype(BF16), preferred_element_type=F32
        ).astype(BF16)
    rows = [b[0] for b in bounds] + [t[0] for t in totals]
    rows += [b[1] for b in bounds] + [t[1] for t in totals]
    out_ref[place + (pl.ds(FEAT, 16), slice(None))] = jnp.concatenate(rows, axis=0).astype(BF16)


def slots_kernel(offsets, first, scal, token, targets, att, bias, *rest):
    del token
    if first:
        sources, (*outs, hidden, made, sems) = rest[:PIECES], rest[PIECES:]
        copies = [
            pltpu.make_async_copy(sources[n], hidden.at[pl.ds(n * NBD, NBD)], sems.at[n])
            for n in range(PIECES)
        ]
        for copy in copies:
            copy.start()
        for copy in copies:
            copy.wait()
    else:
        hidden, *outs, made = rest
    dst = scal[PAIRS + 1]
    together = made.shape[0]

    def some(step, carry):
        for part in range(together):
            for n, offset in enumerate(offsets):
                owner = owner_of(scal, step * together + part, offset)
                for t in range(SLOTS):
                    pair = scal[owner * SLOTS + t]
                    block = pair & (SRC_BLOCKS - 1)
                    place = pair >> (SRC_BLOCKS.bit_length() - 1)
                    holder = block >> (NBD.bit_length() - 1)
                    dx = ((holder >> 1) - (dst >> 1)) & (NX - 1)
                    dc = (holder ^ dst) & (NC - 1)
                    held = ((dx * NC + dc) * NBD) | (block & (NBD - 1))
                    slot_partial(
                        hidden[held], att[...], bias[owner, t].astype(F32), targets[owner, place], made, (part, n, t)
                    )
        for other in range(NY // together):

            @pl.when(step == other)
            def _(other=other):
                for part in range(together):
                    outs[other * together + part][...] = made[part]

        return carry

    lax.fori_loop(0, NY // together, some, 0)


def slots(offsets, scal, token, bias, targets, att, source):
    first = isinstance(source, list)
    shape = (len(offsets), SLOTS, ROWS, BLK)
    out_shape = (jax.ShapeDtypeStruct(shape, BF16),) * NY
    scratch = [pltpu.VMEM((min(NY, 8 // len(offsets)),) + shape, BF16)]
    if first:
        out_shape += (jax.ShapeDtypeStruct((SRC_BLOCKS, FEAT, BLK), BF16),)
        scratch.append(pltpu.SemaphoreType.DMA((PIECES,)))
    return pl.pallas_call(
        functools.partial(slots_kernel, offsets, first),
        out_shape=out_shape,
        in_specs=[SMEM, ANY, VMEM, VMEM, VMEM] + ([ANY] * PIECES if first else [VMEM]),
        out_specs=(VMEM,) * len(out_shape),
        scratch_shapes=scratch,
        compiler_params=params(),
        cost_estimate=pl.CostEstimate(flops=1000, bytes_accessed=1000, transcendentals=0),
        name="slots",
    )(scal, token, targets, att, bias, *(source if first else [source]))


def bound_total(ref, place):
    rows = ref[place + (pl.ds(FEAT, 16), slice(None))].astype(F32)
    both = rows[:8] + rows[8:]
    return both[:HEADS], both[HEADS:]


def merge(slot_list, dense, bounds, totals, sums, given=None):
    for b in range(NBD):
        top = jnp.full((HEADS, BLK), EMPTY, F32) if given is None else given[0][b]
        for ref in dense:
            top = jnp.maximum(top, bound_total(ref, (b,))[0])
        bounds[b] = top
    for ref, index, place in slot_list:
        bounds[place] = jnp.maximum(bounds[place], bound_total(ref, index)[0])
    for b in range(NBD):
        total = jnp.zeros((HEADS, BLK), F32)
        terms = []
        if given is not None:
            factor = jnp.exp2(given[0][b] - bounds[b])
            total += factor if given[1] is None else given[1][b] * factor
            terms.append((given[2], (b,), factor))
        for ref in dense:
            bound, more = bound_total(ref, (b,))
            factor = jnp.exp2(bound - bounds[b])
            total += more * factor
            terms.append((ref, (b,), factor))
        totals[b] = total
        for h in range(HEADS):
            rows = pl.ds(h * HEAD, HEAD)
            value = jnp.zeros((HEAD, BLK), F32)
            for ref, index, factor in terms:
                value += ref[index + (rows, slice(None))].astype(F32) * factor[h : h + 1]
            sums[b, rows, :] = value
    for ref, index, place in slot_list:
        bound, more = bound_total(ref, index)
        factor = jnp.exp2(bound - bounds[place])
        totals[place] += more * factor
        for h in range(HEADS):
            rows = pl.ds(h * HEAD, HEAD)
            sums[place, rows, :] += (
                ref[index + (rows, slice(None))].astype(F32) * factor[h : h + 1]
            )


def placed(scal, every_pair, offset, refs, n):
    owner = owner_of(scal, 0, offset)
    found = []
    for k in range(NY):
        maker = owner_of(scal, -k, 0)
        for t in range(SLOTS):
            place = every_pair[maker * SLOTS + t, owner] >> (SRC_BLOCKS.bit_length() - 1)
            found.append((refs[k], (n, t), place))
    return found


def write_dense(out, bounds, totals, sums):
    for b in range(NBD):
        out[b, pl.ds(0, FEAT), :] = sums[b].astype(BF16)
        both = halves(jnp.concatenate([bounds[b], totals[b]], axis=0))
        out[b, pl.ds(FEAT, 16), :] = jnp.concatenate(both, axis=0).astype(BF16)


def merge_kernel(work, scal, every_pair, *refs):
    parts, refs = refs[:NY], refs[NY:]
    n_dense = sum(w[1] for w in work)
    dense, refs = refs[:n_dense], refs[n_dense:]
    outs, (bounds, totals, sums) = refs[: len(work)], refs[len(work) :]
    for n, (out, (offset, count)) in enumerate(zip(outs, work, strict=True)):
        mine, dense = dense[:count], dense[count:]
        merge(placed(scal, every_pair, offset, parts, n), mine, bounds, totals, sums)
        write_dense(out, bounds, totals, sums)


SUMS = ((NBD, HEADS, BLK), (NBD, HEADS, BLK), (NBD, FEAT, BLK))
SMEM = pl.BlockSpec(memory_space=pltpu.SMEM)


def merge_group(work, scal, every_pair, parts, dense):
    return pl.pallas_call(
        functools.partial(merge_kernel, work),
        out_shape=(jax.ShapeDtypeStruct((NBD, ROWS, BLK), BF16),) * len(work),
        in_specs=[SMEM] * 2 + [VMEM] * (NY + len(dense)),
        out_specs=(VMEM,) * len(work),
        scratch_shapes=[pltpu.VMEM(shape, F32) for shape in SUMS],
        compiler_params=params(),
        cost_estimate=pl.CostEstimate(flops=1000, bytes_accessed=1000, transcendentals=0),
        name="merge",
    )(scal, every_pair, *parts, *dense)


def home_kernel(n, scal, every_pair, *refs):
    parts, (self_ref, hidden_ref, bounds, totals, sums) = refs[:NY], refs[NY:]
    found = placed(scal, every_pair, 0, parts, n)
    merge(found, (), bounds, totals, sums, (self_ref, None, hidden_ref))


def merge_home(scal, every_pair, parts, self_logit, hidden):
    return pl.pallas_call(
        functools.partial(home_kernel, PLAN[-1].index(0)),
        out_shape=tuple(jax.ShapeDtypeStruct(shape, F32) for shape in SUMS),
        in_specs=[SMEM] * 2 + [VMEM] * (NY + 2),
        out_specs=(VMEM,) * 3,
        compiler_params=params(),
        cost_estimate=pl.CostEstimate(flops=1000, bytes_accessed=1000, transcendentals=0),
        name="merge_home",
    )(scal, every_pair, *parts, self_logit, hidden)


def finish_kernel(*refs):
    dense, refs = refs[:-8], refs[-8:]
    home_bounds, home_totals, home_sums, bias_ref, out, bounds, totals, sums = refs
    merge((), dense, bounds, totals, sums, (home_bounds, home_totals, home_sums))
    for b in range(NBD):
        scale = 1.0 / totals[b]
        value = jnp.concatenate(
            [sums[b, pl.ds(h * HEAD, HEAD), :] * scale[h : h + 1] for h in range(HEADS)], axis=0
        )
        value = value.T + bias_ref[...]
        out[pl.ds(b * BLK, BLK), :] = jnp.where(
            value > 0, value, jnp.exp(jnp.minimum(value, 0.0)) - 1.0
        )


def finish(dense, home, bias):
    return pl.pallas_call(
        finish_kernel,
        out_shape=jax.ShapeDtypeStruct((NBD * BLK, FEAT), F32),
        in_specs=[VMEM] * (len(dense) + 4),
        out_specs=VMEM,
        scratch_shapes=[pltpu.VMEM(shape, F32) for shape in SUMS],
        compiler_params=params(),
        name="finish",
    )(*dense, *home, bias.reshape(1, FEAT))


def slots_list(*args):
    return list(slots(*args))


def body(features, weight, att_src, att_dst, bias, block_pairs, edge_masks):
    masks = edge_masks.reshape(OWNERS, SLOTS, BLK, BLK)
    hidden = jnp.dot(features, weight, preferred_element_type=F32).astype(BF16)
    hidden, own_target, self_logit, att = prepare(hidden, att_src, att_dst)
    along_x = [hidden] + [lax.ppermute(hidden, "dst", x_from(k)) for k in range(1, NX)]

    src = lax.axis_index("src")
    dst = lax.axis_index("dst")
    pairs = block_pairs.reshape(-1)
    scal = jnp.concatenate([pairs, jnp.stack([src, dst]).astype(jnp.int32)])

    row = block_pairs.reshape(OWNERS, SLOTS).T.astype(F32)
    row = jnp.pad(row, ((0, HEADS - SLOTS), (0, BLK - OWNERS)))[None]
    told = jnp.concatenate([own_target, row], axis=0)
    told = lax.all_to_all(jnp.broadcast_to(told[None], (OWNERS,) + told.shape), "src", 0, 0)
    every_pair = told[:, NBD, :SLOTS, :OWNERS].astype(jnp.int32).reshape(OWNERS * SLOTS, OWNERS)

    pieces = []
    for piece in along_x:
        pieces += [piece, lax.ppermute(piece, "dst", core_from(1))]
    masks = mask_bias(masks)
    token = gate(*pieces, masks)

    made, parts = [], []
    source = pieces
    for step, offsets in enumerate(PLAN):
        made.append(slots_list(offsets, scal, token, masks, told, att, source))
        if step == 0:
            source = made[0][NY]
        parts.append(
            [made[-1][0]] + [lax.ppermute(made[-1][k], "src", y_from(-k)) for k in range(1, NY)]
        )
    coming = {offset: () for offset in (0, *NEXT)}
    for step, offsets in enumerate(PLAN):
        work = [(offset, len(coming[offset])) for offset in offsets if offset != 0]
        if not work:
            break
        if PLAN[step + 1 : step + 2] == ((0,),):
            parts[step][0], parts[step + 1][1] = lax.optimization_barrier(
                (parts[step][0], parts[step + 1][1])
            )
        if step == 1:
            parts[1][0], made[3][0] = lax.optimization_barrier((parts[1][0], made[3][0]))
        dense = sum((coming[offset] for offset, _ in work), ())
        sent = merge_group(work, scal, every_pair, parts[step], dense)
        for (offset, _), chunk in zip(work, sent, strict=True):
            hop = lax.ppermute(chunk, "src", z_from(NEXT[offset] - offset))
            coming[NEXT[offset]] += (hop,)
    home = merge_home(scal, every_pair, parts[-1], self_logit, hidden)
    return finish(coming[0], home, bias)


def solution(mesh):
    placed_at = (
        P(("dst", "src"), None),
        P(),
        P(),
        P(),
        P(),
        P("src", "dst", None, None),
        P("src", "dst", None, None, None, None),
    )
    return jax.shard_map(
        body, mesh=mesh, in_specs=placed_at, out_specs=P(("dst", "src"), None), check_vma=False
    )
```
